32 devices in a mesh: groups: 2 (over y), expert: 8 (over z, x), dp: 2 (over core).
Axes of the slice: x: 2, y: 2, z: 4, core: 2. Of those that a mesh axis runs over, the one named last changes fastest.
Arguments:
- out_grad: bfloat16 [4096, 3584], P(('groups', 'expert', 'dp')), parts along dimension 0, may hold values from -6 to 6
- hidden: bfloat16 [4096, 8, 1024], P(('groups', 'expert', 'dp')), parts along dimension 0, may hold values from -0.29882812 to 0.29882812
- routes: int32 [4096, 8], P(('groups', 'expert', 'dp')), parts along dimension 0, may hold values from 0 to 255, as said below
- gates: float32 [4096, 8], P(('groups', 'expert', 'dp')), parts along dimension 0, may hold values from 0.02 to 1
- w_down: bfloat16 [8, 1024, 3584], P('expert', 'dp'), may hold values from -0.1875 to 0.1875
Outputs:
- grad_down: bfloat16 [16, 1024, 3584], P(('groups', 'expert'), 'dp'), parts along dimension 0
- grad_hidden: bfloat16 [4096, 8, 1024], P(('groups', 'expert', 'dp')), parts along dimension 0
- grad_gates: float32 [4096, 8], P(('groups', 'expert', 'dp')), parts along dimension 0
The draws below stay inside these ranges and needn't reach their ends.
There are 2 independent parts, one for each index of `groups`. The reference program is written for one: setup_inputs(seed, part) draws one part's arguments, and reference() takes and returns one part's arrays. A program takes and returns all parts, laid end to end along the dimension named above; an argument that names none is the same for every part. Nothing has to cross between parts.
Inputs may be any that keep to these rules, and one draw needn't show every extreme that they name: `routes`: each row names 8 different ids; ids below 8 are the window's experts. Among the 128 rows of one device (aligned blocks in order), each window expert is named by at most 12 rows, and in every block one same expert is named by exactly 12 rows.
All inputs are finite; a program needn't handle non-finite values.
Results may differ from the reference program's by a relative error of at most 0.005.
Values may be sent and summed in bfloat16 or wider, within the bound.
No kernel may reach another device: no remote copies, remote signals or barrier semaphores. Data moves between devices by JAX's collectives and lax.ppermute only.
A program may use at most 128 MiB of HBM per device.

```python
import math
import jax
import jax.numpy as jnp
from jax import lax

D = 3584
FF = 1024
ROUTED = 256
TOPK = 8
TOK_DEV = 128
MOST = 12
EXPERTS = 8
TOKENS = 2048
N_EXPERT = 8
N_DP = 2


def draw_routes(key, part):
    key = jax.random.fold_in(key, 7)
    blocks = TOKENS // TOK_DEV
    keys = jax.random.split(key, 6)
    first = jax.random.randint(keys[0], (blocks, EXPERTS), 1, MOST + 1)
    second = jax.random.randint(keys[1], (blocks, EXPERTS), 1, MOST + 1)
    loads = jnp.minimum(first, second)
    hottest = jax.random.randint(keys[2], (), 0, EXPERTS)
    second_hot = jax.random.randint(keys[3], (blocks,), 0, EXPERTS)
    labels = jnp.arange(EXPERTS, dtype=jnp.int32)
    full = (labels[None, :] == hottest) | (labels[None, :] == second_hot[:, None])
    loads = jnp.where(full, MOST, loads)
    shifts = jax.random.randint(keys[4], (blocks,), 0, ROUTED - EXPERTS)

    def mix_row(sub_key):
        return jax.random.permutation(sub_key, TOPK).astype(jnp.int32)

    def one_block(block_loads, shift, index):
        entry = jnp.arange(EXPERTS * MOST, dtype=jnp.int32)
        owner = entry // MOST
        valid = entry % MOST < block_loads[owner]
        rank = jnp.cumsum(valid.astype(jnp.int32)) - 1
        row = jnp.where(valid, rank % TOK_DEV, TOK_DEV)
        column = jnp.where(valid, rank // TOK_DEV, 0)
        cells = jnp.arange(TOK_DEV * TOPK, dtype=jnp.int32).reshape(TOK_DEV, TOPK)
        table = EXPERTS + (cells + shift) % (ROUTED - EXPERTS)
        table = table.at[row, column].set(owner, mode='drop')
        row_keys = jax.random.split(jax.random.fold_in(keys[5], index), TOK_DEV)
        mixing = jax.vmap(mix_row)(row_keys)
        return jnp.take_along_axis(table, mixing, axis=1)
    result = jax.vmap(one_block)(loads, shifts, jnp.arange(blocks, dtype=jnp.int32))
    return result.reshape(TOKENS, TOPK).astype(jnp.int32)


def shard_levels(rng, dims, cuts, smallest, largest):
    def one(position, parts):
        steps = jax.random.uniform(jax.random.fold_in(jax.random.fold_in(rng, 6), position), (parts,), jnp.float32, smallest / len(cuts), largest / len(cuts))
        return jnp.repeat(jnp.exp(steps), dims[position] // parts).reshape((-1,) + (1,) * (len(dims) - position - 1))

    level = one(*cuts[0])
    for cut in cuts[1:]:
        level = level * one(*cut)
    return level


def scatter_about(key, dims, width, most, pieces=(), kind=jnp.bfloat16):
    drawn = jax.random.normal(key, dims, jnp.float32) * width
    if len(pieces) > 0:
        drawn = shard_levels(key, dims, pieces, -0.22, 0.18) * drawn
    return jnp.clip(drawn, min=-most, max=most).astype(kind)


def setup_inputs(seed: int = 0, part: int = 0) -> dict:
    streams_of = jax.random.split(jax.random.key(seed), 6)
    own_keys = jax.random.split(jax.random.fold_in(streams_of[5], part), 6)
    out_grad = scatter_about(own_keys[0], (TOKENS, D), 1.0, 6.0, ((0, 16),))
    hidden = scatter_about(own_keys[1], (TOKENS, TOPK, FF), 0.05, 0.29882812, ((0, 16),))
    routes = draw_routes(jax.random.fold_in(jax.random.fold_in(streams_of[5], part), 71), part)
    gates = jnp.clip(jnp.exp(math.log(1.0) - 3.912023 * jax.random.uniform(own_keys[3], (TOKENS, TOPK), jnp.float32) ** shard_levels(own_keys[3], (TOKENS, TOPK), ((0, 16),), -0.2, 0.2)), 0.02, 1.0)
    w_down = scatter_about(streams_of[4], (EXPERTS, FF, D), FF ** -0.5, 0.1875, ((0, 8), (1, 2)))
    return {"out_grad": out_grad, "hidden": hidden, "routes": routes, "gates": gates, "w_down": w_down}


def reference(out_grad, hidden, routes, gates, w_down):
    routed = TOKENS * TOPK
    flat_routes = routes.reshape(-1).astype(jnp.int32)
    flat_gates = gates.reshape(routed, 1)
    flat_hidden = hidden.reshape(routed, FF)
    scaled = (flat_gates * flat_hidden.astype(jnp.float32)).astype(jnp.bfloat16)
    scaled_pad = jnp.concatenate([scaled, jnp.zeros((1, FF), jnp.bfloat16)], 0)
    grad_pad = jnp.concatenate([out_grad, jnp.zeros((1, D), jnp.bfloat16)], 0)
    capacity = MOST * N_EXPERT * N_DP

    def per_expert(expert):
        picked = jnp.nonzero(flat_routes == expert, size=capacity, fill_value=routed)[0].astype(jnp.int32)
        owner = jnp.where(picked < routed, picked // TOPK, TOKENS).astype(jnp.int32)
        rows_grad = grad_pad[owner]
        rows_scaled = scaled_pad[picked]
        weight = w_down[expert]
        unit_grad = jnp.dot(rows_grad, weight.T, preferred_element_type=jnp.float32).astype(jnp.bfloat16)
        weight_grad = jnp.dot(rows_scaled.T, rows_grad, preferred_element_type=jnp.float32).astype(jnp.bfloat16)
        return picked, unit_grad, weight_grad

    picked, unit_grad, grad_down = lax.map(per_expert, jnp.arange(EXPERTS, dtype=jnp.int32))
    route_grad = jnp.zeros((routed + 1, FF), jnp.bfloat16).at[picked.reshape(-1)].set(unit_grad.reshape(-1, FF))
    route_grad = route_grad[:routed].astype(jnp.float32)
    grad_hidden = (flat_gates * route_grad).astype(jnp.bfloat16).reshape(TOKENS, TOPK, FF)
    grad_gates = jnp.sum(flat_hidden.astype(jnp.float32) * route_grad, axis=1).reshape(TOKENS, TOPK)
    return (grad_down, grad_hidden, grad_gates)
```

```python
import functools

import jax
import jax.numpy as jnp
from jax import lax
from jax.experimental import pallas as pl
from jax.experimental.pallas import tpu as pltpu
from jax.sharding import PartitionSpec as P

MOST = 12
ROWS = 16
COLS = 3
EXTRA = ROWS - MOST
BF = jnp.bfloat16
F32 = jnp.float32
MIB = 1 << 20


def params(mib=48, **kw):
    return pltpu.CompilerParams(vmem_limit_bytes=mib * MIB, **kw)


def vmem():
    return pl.BlockSpec(memory_space=pltpu.VMEM)


def partner(index, step, peers):
    if peers & (peers - 1) == 0:
        return index ^ step
    return lax.rem(index + step, peers) if isinstance(index, jax.Array) else (index + step) % peers


def routing(routes_t, peers):
    me = lax.axis_index("expert")
    tokens = routes_t.shape[1]
    hits = [routes_t == partner(me, step, peers) for step in range(peers)]
    member = jnp.concatenate(
        [jnp.max(hit.astype(F32), axis=0, keepdims=True) for hit in hits], axis=0
    )
    earlier = lax.broadcasted_iota(jnp.int32, (tokens, tokens), 0) < lax.broadcasted_iota(
        jnp.int32, (tokens, tokens), 1
    )
    before = jnp.dot(member.astype(BF), earlier.astype(F32).astype(BF), preferred_element_type=F32)
    return hits, jnp.where(member > 0, before, -1.0)


def picks(place, peers, block):
    tokens = place.shape[1]
    row = lax.broadcasted_iota(jnp.int32, (ROWS, tokens), 0)
    wanted = jnp.where(row < MOST, row, row - MOST + EXTRA * block).astype(F32)
    return jnp.concatenate(
        [(place[step : step + 1, :] == wanted).astype(F32) for step in range(peers)], axis=0
    )


def low_rows(rows, width):
    return lax.broadcasted_iota(jnp.int32, (rows, width), 0) % ROWS < MOST


def pack_grad(peers, routes_ref, grad_ref, *out_refs):
    _, place = routing(routes_ref[...], peers)
    quarter = grad_ref.shape[1] // 4
    tokens = grad_ref.shape[0]
    low = low_rows(peers * ROWS, tokens)
    last = grad_ref[:, COLS * quarter :]
    for block in range(COLS):
        pick = picks(place, peers, block)
        both = jnp.concatenate(
            [jnp.where(low, pick, 0.0).astype(BF), jnp.where(low, 0.0, pick).astype(BF)], axis=1
        )
        columns = slice(block * quarter, (block + 1) * quarter)
        source = jnp.concatenate([grad_ref[:, columns], last], axis=0)
        packed = jnp.dot(both, source, preferred_element_type=F32).astype(BF)
        for step in range(peers):
            out_refs[step][:, columns] = packed[step * ROWS : (step + 1) * ROWS, :]


def gate_of(hits, gates_t):
    return jnp.concatenate(
        [jnp.sum(jnp.where(hit, gates_t, 0.0), axis=0, keepdims=True) for hit in hits], axis=0
    )


def choice_of(hits):
    return jnp.concatenate(
        [
            jnp.sum(
                jnp.where(hit, lax.broadcasted_iota(jnp.int32, hit.shape, 0).astype(F32), 0.0),
                axis=0,
                keepdims=True,
            )
            for hit in hits
        ],
        axis=0,
    )


def spread(table, pick, peers):
    return jnp.concatenate(
        [
            jnp.sum(
                pick[step * ROWS : (step + 1) * ROWS, :] * table[step : step + 1, :],
                axis=1,
                keepdims=True,
            )
            for step in range(peers)
        ],
        axis=0,
    )


def route_picks(pick, choice, top_count):
    tokens = pick.shape[1]
    routed = tokens * top_count
    token = lax.broadcasted_iota(jnp.int32, (tokens, routed), 0)
    column = lax.broadcasted_iota(jnp.int32, (tokens, routed), 1)
    wide = (column // top_count == token).astype(F32).astype(BF)
    mine = jnp.dot(pick.astype(BF), wide, preferred_element_type=F32)
    which = (
        lax.broadcasted_iota(jnp.int32, (pick.shape[0], routed), 1) % top_count
    ).astype(F32)
    return jnp.where(which == choice, mine, 0.0)


def pack_hidden(peers, routes_ref, gates_ref, hidden_ref, raw_ref, *out_refs):
    hits, place = routing(routes_ref[...], peers)
    gate = gate_of(hits, gates_ref[...])
    choice = choice_of(hits)
    quarter = hidden_ref.shape[1] // 4
    low = low_rows(peers * ROWS, quarter)
    last = hidden_ref[:, COLS * quarter :]
    for block in range(COLS):
        pick = picks(place, peers, block)
        take = route_picks(pick, spread(choice, pick, peers), routes_ref.shape[0]).astype(BF)
        columns = slice(block * quarter, (block + 1) * quarter)
        first = jnp.dot(take, hidden_ref[:, columns], preferred_element_type=F32)
        rest = jnp.dot(take, last, preferred_element_type=F32)
        raw = jnp.where(low, first, rest)
        raw_ref[:, columns] = raw.astype(BF)
        scaled = (spread(gate, pick, peers) * raw).astype(BF)
        for step in range(peers):
            out_refs[step][:, columns] = scaled[step * ROWS : (step + 1) * ROWS, :]


def last_quarter(peers, block):
    rows = peers * ROWS
    to = lax.broadcasted_iota(jnp.int32, (rows, rows), 0)
    at = lax.broadcasted_iota(jnp.int32, (rows, rows), 1)
    inside = at % ROWS
    wanted = at - inside + inside - MOST + EXTRA * block
    return ((inside >= MOST) & (to == wanted)).astype(F32).astype(BF)


def stack(refs, columns):
    return jnp.concatenate([ref[:, columns] for ref in refs], axis=0)


def unpack_last(peers, parts):
    moves = jnp.concatenate([last_quarter(peers, block) for block in range(COLS)], axis=1)
    return jnp.dot(moves, jnp.concatenate(parts, axis=0), preferred_element_type=F32).astype(BF)


def unit_grads(peers, tiles, *refs):
    in_refs, own_ref, other_ref = refs[:peers], refs[peers], refs[peers + 1]
    all_ref, out_refs, quarters_ref = refs[peers + 2], refs[peers + 3 : -1], refs[-1]
    tile = pl.program_id(0)
    quarter = all_ref.shape[1] // 4

    @pl.when(tile == 0)
    def _():
        parts = []
        for block in range(COLS):
            columns = slice(block * quarter, (block + 1) * quarter)
            part = stack(in_refs, columns)
            all_ref[:, columns] = part
            parts.append(part)
        all_ref[:, COLS * quarter :] = unpack_last(peers, parts)

    where = lax.rem(tile + lax.axis_index("dp") * (tiles // 2), tiles)

    def one(weight):
        quarters_ref[where] = lax.dot_general(
            all_ref[...], weight, (((1,), (1,)), ((), ())), preferred_element_type=F32
        ).astype(BF)

    @pl.when(tile < tiles // 2)
    def _():
        one(own_ref[0])

    @pl.when(tile >= tiles // 2)
    def _():
        one(other_ref[0])

    @pl.when(tile == tiles - 1)
    def _():
        width = quarters_ref.shape[2]
        low = low_rows(peers * ROWS, width)
        last = quarters_ref[COLS]
        for block in range(COLS):
            moved = lax.dot_general(
                last_quarter(peers, block),
                last,
                (((0,), (0,)), ((), ())),
                preferred_element_type=F32,
            )
            packed = jnp.where(low, quarters_ref[block].astype(F32), moved).astype(BF)
            for step in range(peers):
                out_refs[step][:, block * width : (block + 1) * width] = packed[
                    step * ROWS : (step + 1) * ROWS, :
                ]


def split_hidden(peers, *refs):
    in_refs, keep_ref, give_ref = refs[:peers], refs[peers], refs[peers + 1]
    quarter = keep_ref.shape[1] // 2
    low = low_rows(peers * ROWS, quarter)
    parts = [stack(in_refs, slice(b * quarter, (b + 1) * quarter)) for b in range(COLS)]
    whole = [jnp.where(low, part.astype(F32), 0.0).astype(BF) for part in parts]
    whole.append(unpack_last(peers, parts))
    half = lax.axis_index("dp") == 0
    for place in range(2):
        columns = slice(place * quarter, (place + 1) * quarter)
        first, second = whole[place].astype(F32), whole[place + 2].astype(F32)
        keep_ref[:, columns] = jnp.where(half, first, second).astype(BF)
        give_ref[:, columns] = jnp.where(half, second, first).astype(BF)


def weight_grad(keep_ref, kept_ref, own_ref, other_ref, out_ref):
    left = jnp.concatenate([keep_ref[...], kept_ref[...]], axis=0)
    right = jnp.concatenate([own_ref[...], other_ref[...]], axis=0)
    out_ref[0] = lax.dot_general(
        left, right, (((0,), (0,)), ((), ())), preferred_element_type=F32
    ).astype(BF)


def finish(peers, routes_ref, gates_ref, raw_ref, *refs):
    in_refs, hidden_ref, gate_ref = refs[:peers], refs[peers], refs[peers + 1]
    hits, place = routing(routes_ref[...], peers)
    gate = gate_of(hits, gates_ref[...])
    choice = choice_of(hits)
    top_count = routes_ref.shape[0]
    quarter = hidden_ref.shape[1] // 4
    rows = peers * ROWS
    routed = hidden_ref.shape[0]
    low = low_rows(rows, routed)
    total = jnp.zeros(gate_ref.shape, F32)
    ways, sent = [], []
    for block in range(COLS):
        columns = slice(block * quarter, (block + 1) * quarter)
        back = stack(in_refs, columns).astype(F32)
        pick = picks(place, peers, block)
        chosen = spread(choice, pick, peers)
        take = route_picks(pick, chosen, top_count)
        down = (((0,), (0,)), ((), ()))
        scaled = (spread(gate, pick, peers) * back).astype(BF)
        hidden_ref[:, columns] = lax.dot_general(
            jnp.where(low, take, 0.0).astype(BF), scaled, down, preferred_element_type=F32
        ).astype(BF)
        ways.append(jnp.where(low, 0.0, take).astype(BF))
        sent.append(scaled)
        value = jnp.sum(raw_ref[:, columns].astype(F32) * back, axis=1, keepdims=True)
        lines = [
            jnp.sum(jnp.where(chosen == float(k), pick * value, 0.0), axis=0, keepdims=True)
            for k in range(top_count)
        ]
        total = total + jnp.concatenate(lines, axis=0)
    hidden_ref[:, COLS * quarter :] = lax.dot_general(
        jnp.concatenate(ways, axis=0),
        jnp.concatenate(sent, axis=0),
        (((0,), (0,)), ((), ())),
        preferred_element_type=F32,
    ).astype(BF)
    gate_ref[...] = total


def local(out_grad, hidden, routes, gates, w_down):
    tokens, top_count = routes.shape
    units = hidden.shape[2]
    width = out_grad.shape[1]
    half = w_down.shape[1]
    routed = tokens * top_count
    peers = lax.axis_size("expert")
    rows = peers * ROWS
    routes_t, gates_t = routes.T, gates.T
    shape = jax.ShapeDtypeStruct
    packed_grad = [shape((ROWS, COLS * width // 4), BF)] * peers
    packed_units = [shape((ROWS, COLS * units // 4), BF)] * peers

    def across(array, step, back=False):
        pairs = [(i, partner(i, step, peers)) for i in range(peers)]
        return lax.ppermute(array, "expert", [(b, a) for a, b in pairs] if back else pairs)

    def swap(array):
        return lax.ppermute(array, "dp", [(0, 1), (1, 0)])

    send_grad = pl.pallas_call(
        functools.partial(pack_grad, peers),
        out_shape=packed_grad,
        in_specs=[vmem()] * 2,
        out_specs=[vmem()] * peers,
        compiler_params=params(),
        name="pack_grad",
    )(routes_t, out_grad)
    recv_grad = [send_grad[0]] + [across(send_grad[s], s) for s in range(1, peers)]
    w_other = swap(w_down)
    raw, *send_units = pl.pallas_call(
        functools.partial(pack_hidden, peers),
        out_shape=[shape((rows, COLS * units // 4), BF)] + packed_units,
        in_specs=[vmem()] * 3,
        out_specs=[vmem()] * (peers + 1),
        compiler_params=params(),
        name="pack_hidden",
    )(routes_t, gates_t, hidden.reshape(routed, units))
    recv_units = [send_units[0]] + [across(send_units[s], s) for s in range(1, peers)]
    tiles = 4
    whole = lambda *dims: pl.BlockSpec(dims, lambda i: (0,) * len(dims))
    all_grad, *unit_out = pl.pallas_call(
        functools.partial(unit_grads, peers, tiles),
        grid=(tiles,),
        out_shape=[shape((rows, width), BF)] + packed_units,
        in_specs=[whole(ROWS, COLS * width // 4)] * peers
        + [
            pl.BlockSpec((1, units // tiles, width), lambda i: (0, jnp.minimum(i, tiles // 2 - 1), 0)),
            pl.BlockSpec((1, units // tiles, width), lambda i: (0, jnp.maximum(i - tiles // 2, 0), 0)),
        ],
        out_specs=[whole(rows, width)] + [whole(ROWS, COLS * units // 4)] * peers,
        scratch_shapes=[pltpu.VMEM((tiles, rows, units // tiles), BF)],
        compiler_params=params(),
        name="unit_grads",
    )(*recv_grad, w_down, w_other)
    back = [unit_out[0]] + [across(unit_out[s], s, True) for s in range(1, peers)]
    other_grad = swap(all_grad)
    keep, give = pl.pallas_call(
        functools.partial(split_hidden, peers),
        out_shape=[shape((rows, half), BF)] * 2,
        in_specs=[vmem()] * peers,
        out_specs=[vmem()] * 2,
        compiler_params=params(),
        name="split_hidden",
    )(*recv_units)
    kept = swap(give)
    strip = 896 if width % 896 == 0 else width
    grad_down = pl.pallas_call(
        weight_grad,
        grid=(width // strip,),
        out_shape=shape((1, half, width), BF),
        in_specs=[whole(rows, half)] * 2 + [pl.BlockSpec((rows, strip), lambda i: (0, i))] * 2,
        out_specs=pl.BlockSpec((1, half, strip), lambda i: (0, 0, i)),
        compiler_params=params(),
        name="weight_grad",
    )(keep, kept, all_grad, other_grad)
    grad_hidden, grad_gates_t = pl.pallas_call(
        functools.partial(finish, peers),
        out_shape=[shape((routed, units), BF), shape((top_count, tokens), F32)],
        in_specs=[vmem()] * (peers + 3),
        out_specs=[vmem()] * 2,
        compiler_params=params(),
        name="finish",
    )(routes_t, gates_t, raw, *back)
    return grad_down, grad_hidden.reshape(tokens, top_count, units), grad_gates_t.T


def solution(mesh):
    in_specs = (
        P(("groups", "expert", "dp"), None),
        P(("groups", "expert", "dp"), None, None),
        P(("groups", "expert", "dp"), None),
        P(("groups", "expert", "dp"), None),
        P("expert", "dp", None),
    )
    out_specs = (
        P(("groups", "expert"), "dp", None),
        P(("groups", "expert", "dp"), None, None),
        P(("groups", "expert", "dp"), None),
    )
    return jax.shard_map(local, mesh=mesh, in_specs=in_specs, out_specs=out_specs, check_vma=False)
```

```python
import functools

import jax
import jax.numpy as jnp
from jax import lax
from jax.experimental import pallas as pl
from jax.experimental.pallas import tpu as pltpu
from jax.sharding import PartitionSpec as P

MOST = 12
ROWS = 16
COLS = 3
EXTRA = ROWS - MOST
BF = jnp.bfloat16
F32 = jnp.float32
MIB = 1 << 20
DOWN = (((0,), (0,)), ((), ()))


FREE = pl.CostEstimate(flops=0, bytes_accessed=0, transcendentals=0)


def params(mib=20, **kw):
    return pltpu.CompilerParams(vmem_limit_bytes=mib * MIB, **kw)


def vmem():
    return pl.BlockSpec(memory_space=pltpu.VMEM)


def anywhere():
    return pl.BlockSpec(memory_space=pl.ANY)


def partner(index, step, peers):
    if peers & (peers - 1) == 0:
        return index ^ step
    return lax.rem(index + step, peers) if isinstance(index, jax.Array) else (index + step) % peers


def routing(routes_t, peers):
    me = lax.axis_index("expert")
    tokens = routes_t.shape[1]
    hits = [routes_t == partner(me, step, peers) for step in range(peers)]
    member = jnp.concatenate(
        [jnp.max(hit.astype(F32), axis=0, keepdims=True) for hit in hits], axis=0
    )
    earlier = lax.broadcasted_iota(jnp.int32, (tokens, tokens), 0) < lax.broadcasted_iota(
        jnp.int32, (tokens, tokens), 1
    )
    before = jnp.dot(member.astype(BF), earlier.astype(F32).astype(BF), preferred_element_type=F32)
    return hits, jnp.where(member > 0, before, -1.0)


def picks(place, peers, block):
    tokens = place.shape[1]
    row = lax.broadcasted_iota(jnp.int32, (ROWS, tokens), 0)
    wanted = jnp.where(row < MOST, row, row - MOST + EXTRA * block).astype(F32)
    return jnp.concatenate(
        [(place[step : step + 1, :] == wanted).astype(F32) for step in range(peers)], axis=0
    )


def low_rows(rows, width):
    return lax.broadcasted_iota(jnp.int32, (rows, width), 0) % ROWS < MOST


def gate_of(hits, gates_t):
    return jnp.concatenate(
        [jnp.sum(jnp.where(hit, gates_t, 0.0), axis=0, keepdims=True) for hit in hits], axis=0
    )


def choice_of(hits):
    return jnp.concatenate(
        [
            jnp.sum(
                jnp.where(hit, lax.broadcasted_iota(jnp.int32, hit.shape, 0).astype(F32), 0.0),
                axis=0,
                keepdims=True,
            )
            for hit in hits
        ],
        axis=0,
    )


def spread(table, pick, peers):
    return jnp.concatenate(
        [
            jnp.sum(
                pick[step * ROWS : (step + 1) * ROWS, :] * table[step : step + 1, :],
                axis=1,
                keepdims=True,
            )
            for step in range(peers)
        ],
        axis=0,
    )


def route_picks(pick, choice, top_count):
    tokens = pick.shape[1]
    routed = tokens * top_count
    token = lax.broadcasted_iota(jnp.int32, (tokens, routed), 0)
    column = lax.broadcasted_iota(jnp.int32, (tokens, routed), 1)
    wide = (column // top_count == token).astype(F32).astype(BF)
    mine = jnp.dot(pick.astype(BF), wide, preferred_element_type=F32)
    which = (lax.broadcasted_iota(jnp.int32, (pick.shape[0], routed), 1) % top_count).astype(F32)
    return jnp.where(which == choice, mine, 0.0)


def pack(peers, *refs):
    sources, raw_ref, out_refs = refs[:4], refs[4], refs[5 : 5 + peers]
    held, sems = refs[5 + peers : -1], refs[-1]
    copies = [
        pltpu.make_async_copy(source, target, sems.at[index])
        for index, (source, target) in enumerate(zip(sources, held))
    ]
    for copy in copies:
        copy.start()
    for copy in copies:
        copy.wait()
    routes_ref, gates_ref, grad_ref, hidden_ref = held
    hits, place = routing(routes_ref[...], peers)
    gate = gate_of(hits, gates_ref[...])
    choice = choice_of(hits)
    tokens = grad_ref.shape[0]
    wide, quarter = grad_ref.shape[1] // 4, hidden_ref.shape[1] // 4
    low = low_rows(peers * ROWS, tokens)
    low_units = low_rows(peers * ROWS, quarter)
    last = grad_ref[:, COLS * wide :]
    last_units = hidden_ref[:, COLS * quarter :]
    for block in range(COLS):
        pick = picks(place, peers, block)
        both = jnp.concatenate(
            [jnp.where(low, pick, 0.0).astype(BF), jnp.where(low, 0.0, pick).astype(BF)], axis=1
        )
        columns = slice(block * wide, (block + 1) * wide)
        source = jnp.concatenate([grad_ref[:, columns], last], axis=0)
        packed = jnp.dot(both, source, preferred_element_type=F32).astype(BF)
        for step in range(peers):
            out_refs[step][:, columns] = packed[step * ROWS : (step + 1) * ROWS, :]
        take = route_picks(pick, spread(choice, pick, peers), routes_ref.shape[0]).astype(BF)
        columns = slice(block * quarter, (block + 1) * quarter)
        first = jnp.dot(take, hidden_ref[:, columns], preferred_element_type=F32)
        rest = jnp.dot(take, last_units, preferred_element_type=F32)
        raw = jnp.where(low_units, first, rest)
        raw_ref[:, columns] = raw.astype(BF)
        scaled = (spread(gate, pick, peers) * raw).astype(BF)
        columns = slice(COLS * wide + block * quarter, COLS * wide + (block + 1) * quarter)
        for step in range(peers):
            out_refs[step][:, columns] = scaled[step * ROWS : (step + 1) * ROWS, :]


def maps(peers, routes_ref, gates_ref, low_ref, high_ref, pick_ref, side_ref):
    hits, place = routing(routes_ref[...], peers)
    gate = gate_of(hits, gates_ref[...])
    choice = choice_of(hits)
    rows = peers * ROWS
    routed = low_ref.shape[0]
    low = low_rows(rows, routed)
    side_ref[...] = jnp.zeros_like(side_ref)
    for block in range(COLS):
        pick = picks(place, peers, block)
        chosen = spread(choice, pick, peers)
        take = route_picks(pick, chosen, routes_ref.shape[0])
        if block == 0:
            low_ref[...] = jnp.where(low, take, 0.0).T.astype(BF)
        high_ref[:, block * rows : (block + 1) * rows] = jnp.where(low, 0.0, take).T.astype(BF)
        pick_ref[block] = pick
        side_ref[:, block : block + 1] = spread(gate, pick, peers)
        side_ref[:, COLS + block : COLS + block + 1] = chosen


def last_quarter(peers, block):
    rows = peers * ROWS
    to = lax.broadcasted_iota(jnp.int32, (rows, rows), 0)
    at = lax.broadcasted_iota(jnp.int32, (rows, rows), 1)
    inside = at % ROWS
    wanted = at - MOST + EXTRA * block
    return ((inside >= MOST) & (to == wanted)).astype(F32).astype(BF)


def stack(refs, columns):
    return jnp.concatenate([ref[:, columns] for ref in refs], axis=0)


def unpack_last(peers, parts):
    moves = jnp.concatenate([last_quarter(peers, block) for block in range(COLS)], axis=1)
    return jnp.dot(moves, jnp.concatenate(parts, axis=0), preferred_element_type=F32).astype(BF)


def unit_grads(count, extra, *refs):
    in_refs, own_ref, other_ref = refs[:count], refs[count], refs[count + 1]
    refs = refs[: count + 2] + refs[count + 2 + extra :]
    swap_ref, keep_ref = refs[count + 2], refs[count + 3]
    out_refs = refs[count + 4 : 2 * count + 4]
    half_units, width = own_ref.shape[1], own_ref.shape[2]
    quarter, wide = half_units // 2, width // 4
    rows = count * ROWS
    first_core = lax.axis_index("dp") == 0
    parts = []
    for block in range(COLS):
        part = stack(in_refs, slice(block * wide, (block + 1) * wide))
        swap_ref[:, block * wide : (block + 1) * wide] = part
        parts.append(part)
    swap_ref[:, COLS * wide : 4 * wide] = unpack_last(count, parts)
    left = swap_ref[:, : 4 * wide]
    across = (((1,), (1,)), ((), ()))
    halves = [
        lax.dot_general(left, ref[0], across, preferred_element_type=F32)
        for ref in (own_ref, other_ref)
    ]
    low_half = jnp.where(first_core, halves[0], halves[1])
    high_half = jnp.where(first_core, halves[1], halves[0])
    units = [low_half[:, :quarter], low_half[:, quarter:], high_half[:, :quarter]]
    last = high_half[:, quarter:].astype(BF)
    low = low_rows(rows, quarter)
    for block in range(COLS):
        moved = lax.dot_general(
            last_quarter(count, block), last, DOWN, preferred_element_type=F32
        )
        packed = jnp.where(low, units[block], moved).astype(BF)
        for step in range(count):
            out_refs[step][:, block * quarter : (block + 1) * quarter] = packed[
                step * ROWS : (step + 1) * ROWS, :
            ]
    start = COLS * wide
    parts = [
        stack(in_refs, slice(start + b * quarter, start + (b + 1) * quarter)) for b in range(COLS)
    ]
    scaled = [jnp.where(low, part.astype(F32), 0.0) for part in parts]
    scaled.append(unpack_last(count, parts).astype(F32))
    for place in range(2):
        one, two = scaled[place], scaled[place + 2]
        keep_ref[:, place * quarter : (place + 1) * quarter] = jnp.where(
            first_core, one, two
        ).astype(BF)
        swap_ref[:, width + place * quarter : width + (place + 1) * quarter] = jnp.where(
            first_core, two, one
        ).astype(BF)


def weight_grad(groups, strip, *refs):
    keep_refs, own_refs, other_refs = (refs[i * groups : (i + 1) * groups] for i in range(3))
    out_ref, done_ref, held, sems = refs[3 * groups :]
    done_ref[...] = jnp.zeros_like(done_ref)
    width = out_ref.shape[2]
    half = out_ref.shape[1]
    left = jnp.concatenate(
        [ref[...] for ref in keep_refs] + [ref[:, width : width + half] for ref in other_refs], axis=0
    )
    copies = []
    for index in range(width // strip):
        columns = slice(index * strip, (index + 1) * strip)
        right = jnp.concatenate([ref[:, columns] for ref in (*own_refs, *other_refs)], axis=0)
        slot = index % 2
        if index >= 2:
            copies[index - 2].wait()
        held[slot] = lax.dot_general(left, right, DOWN, preferred_element_type=F32).astype(BF)
        copy = pltpu.make_async_copy(held.at[slot], out_ref.at[0, :, columns], sems.at[slot])
        copy.start()
        copies.append(copy)
    for copy in copies[-2:]:
        copy.wait()


def finish(peers, pieces, low_ref, high_ref, pick_ref, side_ref, raw_ref, *refs):
    in_refs, (hidden_ref, gate_ref, held, sems) = refs[:peers], refs[peers + 1 :]
    top_count = gate_ref.shape[0]
    routed, units = hidden_ref.shape
    quarter = units // 4
    total = jnp.zeros(gate_ref.shape, F32)
    sent = []
    for block in range(COLS):
        columns = slice(block * quarter, (block + 1) * quarter)
        back = stack(in_refs, columns).astype(F32)
        sent.append((side_ref[:, block : block + 1] * back).astype(BF))
        value = jnp.sum(raw_ref[:, columns].astype(F32) * back, axis=1, keepdims=True)
        chosen = side_ref[:, COLS + block : COLS + block + 1]
        weighted = pick_ref[block] * value
        lines = [
            jnp.sum(jnp.where(chosen == float(k), weighted, 0.0), axis=0, keepdims=True)
            for k in range(top_count)
        ]
        total = total + jnp.concatenate(lines, axis=0)
    stacked = jnp.concatenate(sent, axis=0)
    size = routed // pieces
    copies = []
    for piece in range(pieces):
        at = slice(piece * size, (piece + 1) * size)
        for block in range(COLS):
            held[at, block * quarter : (block + 1) * quarter] = jnp.dot(
                low_ref[at, :], sent[block], preferred_element_type=F32
            ).astype(BF)
        held[at, COLS * quarter :] = jnp.dot(
            high_ref[at, :], stacked, preferred_element_type=F32
        ).astype(BF)
        copy = pltpu.make_async_copy(held.at[at], hidden_ref.at[at], sems.at[piece])
        copy.start()
        copies.append(copy)
    gate_ref[...] = total
    for copy in copies:
        copy.wait()


def local(out_grad, hidden, routes, gates, w_down):
    tokens, top_count = routes.shape
    units = hidden.shape[2]
    width = out_grad.shape[1]
    half = w_down.shape[1]
    routed = tokens * top_count
    peers = lax.axis_size("expert")
    rows = peers * ROWS
    routes_t, gates_t = routes.T, gates.T
    shape = jax.ShapeDtypeStruct
    near = list(range(peers // 2))
    far = list(range(peers // 2, peers))
    batches = [near, far]
    order = far[:1] + near[1:] + far[1:]

    def across(array, step, back=False):
        pairs = [(i, partner(i, step, peers)) for i in range(peers)]
        return lax.ppermute(array, "expert", [(b, a) for a, b in pairs] if back else pairs)

    def swap(array):
        return lax.ppermute(array, "dp", [(0, 1), (1, 0)])

    w_other = swap(w_down)
    raw, *sent = pl.pallas_call(
        functools.partial(pack, peers),
        out_shape=[shape((rows, COLS * units // 4), BF)]
        + [shape((ROWS, COLS * (units + width) // 4), BF)] * peers,
        in_specs=[pl.BlockSpec(memory_space=pltpu.HBM)] * 4,
        out_specs=[vmem()] * (peers + 1),
        scratch_shapes=[
            pltpu.VMEM((top_count, tokens), jnp.int32),
            pltpu.VMEM((top_count, tokens), F32),
            pltpu.VMEM((tokens, width), BF),
            pltpu.VMEM((routed, units), BF),
            pltpu.SemaphoreType.DMA((4,)),
        ],
        compiler_params=params(58),
        name="pack",
        cost_estimate=FREE,
    )(routes_t, gates_t, out_grad, hidden.reshape(routed, units))
    received = {0: sent[0]}
    for step in order:
        received[step] = across(sent[step], step)
    low_map, high_map, pick_map, side = pl.pallas_call(
        functools.partial(maps, peers),
        out_shape=[
            shape((routed, rows), BF),
            shape((routed, COLS * rows), BF),
            shape((COLS, rows, tokens), F32),
            shape((rows, 128), F32),
        ],
        in_specs=[vmem()] * 2,
        out_specs=[vmem()] * 4,
        compiler_params=params(),
        name="maps",
        cost_estimate=FREE,
    )(routes_t, gates_t)
    keeps, owns, others, back = [], [], [], {}
    for batch in batches:
        count = len(batch)
        after = [pick_map] + [back[step] for step in back if step]
        own, keep, *out = pl.pallas_call(
            functools.partial(unit_grads, count, len(after)),
            out_shape=[
                shape((count * ROWS, width + half), BF),
                shape((count * ROWS, half), BF),
            ]
            + [shape((ROWS, COLS * units // 4), BF)] * count,
            in_specs=[vmem()] * (count + 2) + [anywhere()] * len(after),
            out_specs=[vmem()] * (count + 2),
            compiler_params=params(),
            name="unit_grads",
            cost_estimate=FREE,
        )(*[received[step] for step in batch], w_down, w_other, *after)
        for step, array in zip(batch, out):
            back[step] = array if step == 0 else across(array, step, True)
        keeps.append(keep)
        owns.append(own)
        others.append(swap(own))
    strip = 512 if width % 512 == 0 else width
    grad_down, done = pl.pallas_call(
        functools.partial(weight_grad, len(batches), strip),
        out_shape=[shape((1, half, width), BF), shape((8, 128), F32)],
        in_specs=[vmem()] * (3 * len(batches)),
        out_specs=[anywhere(), vmem()],
        scratch_shapes=[pltpu.VMEM((2, half, strip), BF), pltpu.SemaphoreType.DMA((2,))],
        compiler_params=params(),
        name="weight_grad",
    )(*keeps, *owns, *others)
    pieces = 4
    grad_hidden, grad_gates_t = pl.pallas_call(
        functools.partial(finish, peers, pieces),
        out_shape=[shape((routed, units), BF), shape((top_count, tokens), F32)],
        in_specs=[vmem()] * (peers + 5) + [anywhere()],
        out_specs=[anywhere(), vmem()],
        scratch_shapes=[pltpu.VMEM((routed, units), BF), pltpu.SemaphoreType.DMA((pieces,))],
        compiler_params=params(),
        name="finish",
    )(low_map, high_map, pick_map, side, raw, *[back[step] for step in range(peers)], done)
    return grad_down, grad_hidden.reshape(tokens, top_count, units), grad_gates_t.T


def solution(mesh):
    in_specs = (
        P(("groups", "expert", "dp"), None),
        P(("groups", "expert", "dp"), None, None),
        P(("groups", "expert", "dp"), None),
        P(("groups", "expert", "dp"), None),
        P("expert", "dp", None),
    )
    out_specs = (
        P(("groups", "expert"), "dp", None),
        P(("groups", "expert", "dp"), None, None),
        P(("groups", "expert", "dp"), None),
    )
    return jax.shard_map(local, mesh=mesh, in_specs=in_specs, out_specs=out_specs, check_vma=False)
```

```python
import functools

import jax
import jax.numpy as jnp
from jax import lax
from jax.experimental import pallas as pl
from jax.experimental.pallas import tpu as pltpu
from jax.sharding import PartitionSpec as P

MOST = 12
ROWS = 16
COLS = 3
EXTRA = ROWS - MOST
BF = jnp.bfloat16
F32 = jnp.float32
MIB = 1 << 20
DOWN = (((0,), (0,)), ((), ()))


FREE = pl.CostEstimate(flops=0, bytes_accessed=0, transcendentals=0)


def params(mib=20, **kw):
    return pltpu.CompilerParams(vmem_limit_bytes=mib * MIB, **kw)


def vmem():
    return pl.BlockSpec(memory_space=pltpu.VMEM)


def anywhere():
    return pl.BlockSpec(memory_space=pl.ANY)


def partner(index, step, peers):
    if peers & (peers - 1) == 0:
        return index ^ step
    return lax.rem(index + step, peers) if isinstance(index, jax.Array) else (index + step) % peers


def routing(routes_t, peers, steps):
    me = lax.axis_index("expert")
    tokens = routes_t.shape[1]
    hits = [routes_t == partner(me, step, peers) for step in steps]
    member = jnp.concatenate(
        [jnp.max(hit.astype(F32), axis=0, keepdims=True) for hit in hits], axis=0
    )
    earlier = lax.broadcasted_iota(jnp.int32, (tokens, tokens), 0) < lax.broadcasted_iota(
        jnp.int32, (tokens, tokens), 1
    )
    before = jnp.dot(member.astype(BF), earlier.astype(F32).astype(BF), preferred_element_type=F32)
    return hits, jnp.where(member > 0, before, -1.0)


def picks(place, block):
    tokens = place.shape[1]
    row = lax.broadcasted_iota(jnp.int32, (ROWS, tokens), 0)
    wanted = jnp.where(row < MOST, row, row - MOST + EXTRA * block).astype(F32)
    return jnp.concatenate(
        [(place[step : step + 1, :] == wanted).astype(F32) for step in range(place.shape[0])], axis=0
    )


def low_rows(rows, width):
    return lax.broadcasted_iota(jnp.int32, (rows, width), 0) % ROWS < MOST


def gate_of(hits, gates_t):
    return jnp.concatenate(
        [jnp.sum(jnp.where(hit, gates_t, 0.0), axis=0, keepdims=True) for hit in hits], axis=0
    )


def choice_of(hits):
    return jnp.concatenate(
        [
            jnp.sum(
                jnp.where(hit, lax.broadcasted_iota(jnp.int32, hit.shape, 0).astype(F32), 0.0),
                axis=0,
                keepdims=True,
            )
            for hit in hits
        ],
        axis=0,
    )


def spread(table, pick):
    return jnp.concatenate(
        [
            jnp.sum(
                pick[step * ROWS : (step + 1) * ROWS, :] * table[step : step + 1, :],
                axis=1,
                keepdims=True,
            )
            for step in range(table.shape[0])
        ],
        axis=0,
    )


def route_picks(pick, choice, top_count):
    tokens = pick.shape[1]
    routed = tokens * top_count
    token = lax.broadcasted_iota(jnp.int32, (tokens, routed), 0)
    column = lax.broadcasted_iota(jnp.int32, (tokens, routed), 1)
    wide = (column // top_count == token).astype(F32).astype(BF)
    mine = jnp.dot(pick.astype(BF), wide, preferred_element_type=F32)
    which = (lax.broadcasted_iota(jnp.int32, (pick.shape[0], routed), 1) % top_count).astype(F32)
    return jnp.where(which == choice, mine, 0.0)


def pack(peers, steps, extra, *refs):
    sources, refs, count = refs[:4], refs[4 + extra :], len(steps)
    raw_ref, out_refs, held, sems = refs[0], refs[1 : 1 + count], refs[1 + count : -1], refs[-1]
    copies = [
        pltpu.make_async_copy(source, target, sems.at[index])
        for index, (source, target) in enumerate(zip(sources, held))
    ]
    for copy in copies:
        copy.start()
    for copy in copies[:3]:
        copy.wait()
    routes_ref, gates_ref, grad_ref, hidden_ref = held
    hits, place = routing(routes_ref[...], peers, steps)
    gate = gate_of(hits, gates_ref[...])
    choice = choice_of(hits)
    tokens = grad_ref.shape[0]
    wide, quarter = grad_ref.shape[1] // 4, hidden_ref.shape[1] // 4
    low = low_rows(count * ROWS, tokens)
    low_units = low_rows(count * ROWS, quarter)
    last = grad_ref[:, COLS * wide :]
    taken = []
    for block in range(COLS):
        pick = picks(place, block)
        both = jnp.concatenate(
            [jnp.where(low, pick, 0.0).astype(BF), jnp.where(low, 0.0, pick).astype(BF)], axis=1
        )
        columns = slice(block * wide, (block + 1) * wide)
        source = jnp.concatenate([grad_ref[:, columns], last], axis=0)
        packed = jnp.dot(both, source, preferred_element_type=F32).astype(BF)
        for step in range(count):
            out_refs[step][:, columns] = packed[step * ROWS : (step + 1) * ROWS, :]
        take = route_picks(pick, spread(choice, pick), routes_ref.shape[0]).astype(BF)
        taken.append((take, spread(gate, pick)))
    copies[3].wait()
    rows = count * ROWS
    first = jnp.dot(taken[0][0], hidden_ref[:, : COLS * quarter], preferred_element_type=F32)
    rest = jnp.dot(
        jnp.concatenate([take for take, _ in taken], axis=0),
        hidden_ref[:, COLS * quarter :],
        preferred_element_type=F32,
    )
    for block, (_, weight) in enumerate(taken):
        columns = slice(block * quarter, (block + 1) * quarter)
        raw = jnp.where(low_units, first[:, columns], rest[block * rows : (block + 1) * rows, :])
        raw_ref[:, columns] = raw.astype(BF)
        scaled = (weight * raw).astype(BF)
        columns = slice(COLS * wide + block * quarter, COLS * wide + (block + 1) * quarter)
        for step in range(count):
            out_refs[step][:, columns] = scaled[step * ROWS : (step + 1) * ROWS, :]


def maps(peers, routes_ref, gates_ref, weight_ref, low_ref, pick_ref, side_ref):
    hits, place = routing(routes_ref[...], peers, range(peers))
    gate, choice = gate_of(hits, gates_ref[...]), choice_of(hits)
    low = low_rows(peers * ROWS, low_ref.shape[0])
    side_ref[...] = jnp.zeros_like(side_ref)
    for block in range(COLS):
        pick = picks(place, block)
        chosen = spread(choice, pick)
        if block == 0:
            take = route_picks(pick, chosen, routes_ref.shape[0])
            low_ref[...] = jnp.where(low, take, 0.0).T.astype(BF)
        pick_ref[block] = pick
        side_ref[:, block : block + 1] = spread(gate, pick)
        side_ref[:, COLS + block : COLS + block + 1] = chosen


def last_quarter(peers, block):
    rows = peers * ROWS
    to = lax.broadcasted_iota(jnp.int32, (rows, rows), 0)
    at = lax.broadcasted_iota(jnp.int32, (rows, rows), 1)
    inside = at % ROWS
    wanted = at - MOST + EXTRA * block
    return ((inside >= MOST) & (to == wanted)).astype(F32).astype(BF)


def block_of(step, peers):
    return pl.ds(pl.multiple_of(partner(lax.axis_index("expert"), step, peers) * ROWS, ROWS), ROWS)


def stack(refs, columns):
    return jnp.concatenate([ref[:, columns] for ref in refs], axis=0)


def unpack_last(peers, parts):
    moves = jnp.concatenate([last_quarter(peers, block) for block in range(COLS)], axis=1)
    return jnp.dot(moves, jnp.concatenate(parts, axis=0), preferred_element_type=F32).astype(BF)


def unit_grads(steps, peers, *refs):
    count, base, extra = len(steps), 0, 1
    in_refs, own_ref, other_ref = refs[:count], refs[count], refs[count + 1]
    refs = refs[count + 2 + extra :]
    here = slice(base * ROWS, (base + count) * ROWS)
    swap_ref, keep_ref = refs[0].at[here], refs[1].at[here]
    out_refs = refs[2:]
    half_units, width = own_ref.shape[1], own_ref.shape[2]
    quarter, wide = half_units // 2, width // 4
    rows = count * ROWS
    first_core = lax.axis_index("dp") == 0
    parts = []
    for block in range(COLS):
        part = stack(in_refs, slice(block * wide, (block + 1) * wide))
        swap_ref[:, block * wide : (block + 1) * wide] = part
        parts.append(part)
    swap_ref[:, COLS * wide : 4 * wide] = unpack_last(count, parts)
    left = swap_ref[:, : 4 * wide]
    across = (((1,), (1,)), ((), ()))
    halves = [
        lax.dot_general(left, ref[0], across, preferred_element_type=F32)
        for ref in (own_ref, other_ref)
    ]
    low_half = jnp.where(first_core, halves[0], halves[1])
    high_half = jnp.where(first_core, halves[1], halves[0])
    units = [low_half[:, :quarter], low_half[:, quarter:], high_half[:, :quarter]]
    last = high_half[:, quarter:].astype(BF)
    low = low_rows(rows, quarter)
    for block in range(COLS):
        moved = lax.dot_general(
            last_quarter(count, block), last, DOWN, preferred_element_type=F32
        )
        packed = jnp.where(low, units[block], moved).astype(BF)
        for index, step in enumerate(steps):
            out_refs[0][block_of(step, peers), block * quarter : (block + 1) * quarter] = packed[
                index * ROWS : (index + 1) * ROWS, :
            ]
    start = COLS * wide
    parts = [
        stack(in_refs, slice(start + b * quarter, start + (b + 1) * quarter)) for b in range(COLS)
    ]
    scaled = [jnp.where(low, part.astype(F32), 0.0) for part in parts]
    scaled.append(unpack_last(count, parts).astype(F32))
    for place in range(2):
        one, two = scaled[place], scaled[place + 2]
        keep_ref[:, place * quarter : (place + 1) * quarter] = jnp.where(
            first_core, one, two
        ).astype(BF)
        swap_ref[:, width + place * quarter : width + (place + 1) * quarter] = jnp.where(
            first_core, two, one
        ).astype(BF)


def weight_grad(strip, keep_ref, own_ref, other_ref, out_ref, done_ref, held, sems):
    done_ref[...] = jnp.zeros_like(done_ref)
    width = out_ref.shape[2]
    half = out_ref.shape[1]
    left = jnp.concatenate([keep_ref[...], other_ref[:, width : width + half]], axis=0).T
    copies = []
    for index in range(width // strip):
        columns = slice(index * strip, (index + 1) * strip)
        right = jnp.concatenate([own_ref[:, columns], other_ref[:, columns]], axis=0)
        held[index] = jnp.dot(left, right, preferred_element_type=F32).astype(BF)
        copy = pltpu.make_async_copy(held.at[index], out_ref.at[0, :, columns], sems.at[index])
        copy.start()
        copies.append(copy)
    for copy in copies:
        copy.wait()


def finish(peers, packs, pieces, low_ref, pick_ref, side_ref, *refs):
    raw_refs, refs = refs[: len(packs)], refs[len(packs) :]
    found = {step: (ref, at) for ref, pack in zip(raw_refs, packs) for at, step in enumerate(pack)}
    back_ref, (hidden_ref, gate_ref, held, sems) = refs[0], refs[2:]
    top_count = gate_ref.shape[0]
    routed, units = hidden_ref.shape
    quarter = units // 4
    backs, sent = [], []
    for block in range(COLS):
        columns = slice(block * quarter, (block + 1) * quarter)
        back = jnp.concatenate(
            [back_ref[block_of(step, peers), columns] for step in range(peers)], axis=0
        ).astype(F32)
        backs.append(back)
        sent.append((side_ref[:, block : block + 1] * back).astype(BF))
    full = jnp.concatenate([*sent, unpack_last(peers, sent)], axis=1)
    size = routed // pieces
    copies = []
    for piece in range(pieces):
        at = slice(piece * size, (piece + 1) * size)
        held[at] = jnp.dot(low_ref[at, :], full, preferred_element_type=F32).astype(BF)
        copy = pltpu.make_async_copy(held.at[at], hidden_ref.at[at], sems.at[piece])
        copy.start()
        copies.append(copy)
    total = jnp.zeros(gate_ref.shape, F32)
    for block, back in enumerate(backs):
        columns = slice(block * quarter, (block + 1) * quarter)
        raws = jnp.concatenate(
            [
                found[step][0][found[step][1] * ROWS : (found[step][1] + 1) * ROWS, columns]
                for step in range(peers)
            ],
            axis=0,
        )
        value = jnp.sum(raws.astype(F32) * back, axis=1, keepdims=True)
        chosen = side_ref[:, COLS + block : COLS + block + 1]
        weighted = pick_ref[block] * value
        lines = [
            jnp.sum(jnp.where(chosen == float(k), weighted, 0.0), axis=0, keepdims=True)
            for k in range(top_count)
        ]
        total = total + jnp.concatenate(lines, axis=0)
    gate_ref[...] = total
    for copy in copies:
        copy.wait()


def local(out_grad, hidden, routes, gates, w_down):
    tokens, top_count = routes.shape
    units = hidden.shape[2]
    width = out_grad.shape[1]
    half = w_down.shape[1]
    routed = tokens * top_count
    peers = lax.axis_size("expert")
    rows = peers * ROWS
    routes_t, gates_t = routes.T, gates.T
    shape = jax.ShapeDtypeStruct
    half_way = peers // 2
    room = 20 if peers <= 8 else 60
    order = [half_way, *range(1, half_way), *range(half_way + 1, peers)]
    packs = [list(range(peers))]

    def across(array, step, back=False):
        pairs = [(i, partner(i, step, peers)) for i in range(peers)]
        return lax.ppermute(array, "expert", [(b, a) for a, b in pairs] if back else pairs)

    def swap(array):
        return lax.ppermute(array, "dp", [(0, 1), (1, 0)])

    w_other = swap(w_down)
    raws, received = [], {-1: w_other}
    for batch in packs:
        after = list(raws)
        count = len(batch)
        raw, *sent = pl.pallas_call(
            functools.partial(pack, peers, batch, len(raws)),
            out_shape=[shape((count * ROWS, COLS * units // 4), BF)]
            + [shape((ROWS, COLS * (units + width) // 4), BF)] * count,
            in_specs=[pl.BlockSpec(memory_space=pltpu.HBM)] * 4 + [anywhere()] * len(raws),
            out_specs=[vmem()] * (count + 1),
            scratch_shapes=[
                pltpu.VMEM((top_count, tokens), jnp.int32),
                pltpu.VMEM((top_count, tokens), F32),
                pltpu.VMEM((tokens, width), BF),
                pltpu.VMEM((routed, units), BF),
                pltpu.SemaphoreType.DMA((4,)),
            ],
            compiler_params=params(56 if peers <= 8 else 60),
            name="pack",
            cost_estimate=FREE,
        )(routes_t, gates_t, out_grad, hidden.reshape(routed, units), *after)
        raws.append(raw)
        received[0] = sent[0]
        chains = {step: -1 for step in range(half_way + 1, peers)}
        for step in order:
            array = sent[step]
            if step in chains:
                array = lax.optimization_barrier((array, received[chains[step]]))[0]
            received[step] = across(array, step)
    low_map, pick_map, side = pl.pallas_call(
        functools.partial(maps, peers),
        out_shape=[
            shape((routed, rows), BF),
            shape((COLS, rows, tokens), F32),
            shape((rows, 128), F32),
        ],
        in_specs=[vmem()] * 3,
        out_specs=[vmem()] * 3,
        compiler_params=params(room),
        name="maps",
        cost_estimate=FREE,
    )(routes_t, gates_t, w_down)
    steps = [*order, 0]
    own, keep, back = pl.pallas_call(
        functools.partial(unit_grads, steps, peers),
        out_shape=[
            shape((rows, width + half), BF),
            shape((rows, half), BF),
            shape((rows, COLS * units // 4), BF),
        ],
        in_specs=[vmem()] * (peers + 2) + [anywhere()],
        out_specs=[vmem()] * 3,
        compiler_params=params(room),
        name="unit_grads",
        cost_estimate=FREE,
    )(*[received[step] for step in steps], w_down, w_other, pick_map)
    other = swap(own)
    back = lax.all_to_all(back, "expert", split_axis=0, concat_axis=0, tiled=True)
    strip = 512 if width % 512 == 0 else width
    grad_down, done = pl.pallas_call(
        functools.partial(weight_grad, strip),
        out_shape=[shape((1, half, width), BF), shape((8, 128), F32)],
        in_specs=[vmem()] * 3,
        out_specs=[anywhere(), vmem()],
        scratch_shapes=[
            pltpu.VMEM((width // strip, half, strip), BF),
            pltpu.SemaphoreType.DMA((width // strip,)),
        ],
        compiler_params=params(room),
        name="weight_grad",
    )(keep, own, other)
    pieces = 4
    grad_hidden, grad_gates_t = pl.pallas_call(
        functools.partial(finish, peers, packs, pieces),
        out_shape=[shape((routed, units), BF), shape((top_count, tokens), F32)],
        in_specs=[vmem()] * (4 + len(packs)) + [anywhere()],
        out_specs=[anywhere(), vmem()],
        scratch_shapes=[pltpu.VMEM((routed, units), BF), pltpu.SemaphoreType.DMA((pieces,))],
        compiler_params=params(room),
        name="finish",
    )(low_map, pick_map, side, *raws, back, done)
    return grad_down, grad_hidden.reshape(tokens, top_count, units), grad_gates_t.T


def solution(mesh):
    in_specs = (
        P(("groups", "expert", "dp"), None),
        P(("groups", "expert", "dp"), None, None),
        P(("groups", "expert", "dp"), None),
        P(("groups", "expert", "dp"), None),
        P("expert", "dp", None),
    )
    out_specs = (
        P(("groups", "expert"), "dp", None),
        P(("groups", "expert", "dp"), None, None),
        P(("groups", "expert", "dp"), None),
    )
    return jax.shard_map(local, mesh=mesh, in_specs=in_specs, out_specs=out_specs, check_vma=False)
```

```python
import functools

import jax
import jax.numpy as jnp
from jax import lax
from jax.experimental import pallas as pl
from jax.experimental.pallas import tpu as pltpu
from jax.sharding import PartitionSpec as P

MOST = 12
ROWS = 16
COLS = 3
EXTRA = ROWS - MOST
BF = jnp.bfloat16
F32 = jnp.float32
MIB = 1 << 20
DOWN = (((0,), (0,)), ((), ()))


FREE = pl.CostEstimate(flops=0, bytes_accessed=0, transcendentals=0)


def params(mib=20, **kw):
    return pltpu.CompilerParams(vmem_limit_bytes=mib * MIB, **kw)


def vmem():
    return pl.BlockSpec(memory_space=pltpu.VMEM)


def anywhere():
    return pl.BlockSpec(memory_space=pl.ANY)


def partner(index, step, peers):
    if peers & (peers - 1) == 0:
        return index ^ step
    return lax.rem(index + step, peers) if isinstance(index, jax.Array) else (index + step) % peers


def routing(routes_t, peers, steps):
    me = lax.axis_index("expert")
    tokens = routes_t.shape[1]
    hits = [routes_t == partner(me, step, peers) for step in steps]
    member = jnp.concatenate(
        [jnp.max(hit.astype(F32), axis=0, keepdims=True) for hit in hits], axis=0
    )
    earlier = lax.broadcasted_iota(jnp.int32, (tokens, tokens), 0) < lax.broadcasted_iota(
        jnp.int32, (tokens, tokens), 1
    )
    before = jnp.dot(member.astype(BF), earlier.astype(F32).astype(BF), preferred_element_type=F32)
    return hits, jnp.where(member > 0, before, -1.0)


def picks(place, block):
    tokens = place.shape[1]
    row = lax.broadcasted_iota(jnp.int32, (ROWS, tokens), 0)
    wanted = jnp.where(row < MOST, row, row - MOST + EXTRA * block).astype(F32)
    return jnp.concatenate(
        [(place[step : step + 1, :] == wanted).astype(F32) for step in range(place.shape[0])], axis=0
    )


def low_rows(rows, width):
    return lax.broadcasted_iota(jnp.int32, (rows, width), 0) % ROWS < MOST


def gate_of(hits, gates_t):
    return jnp.concatenate(
        [jnp.sum(jnp.where(hit, gates_t, 0.0), axis=0, keepdims=True) for hit in hits], axis=0
    )


def choice_of(hits):
    return jnp.concatenate(
        [
            jnp.sum(
                jnp.where(hit, lax.broadcasted_iota(jnp.int32, hit.shape, 0).astype(F32), 0.0),
                axis=0,
                keepdims=True,
            )
            for hit in hits
        ],
        axis=0,
    )


def spread(table, pick):
    return jnp.concatenate(
        [
            jnp.sum(
                pick[step * ROWS : (step + 1) * ROWS, :] * table[step : step + 1, :],
                axis=1,
                keepdims=True,
            )
            for step in range(table.shape[0])
        ],
        axis=0,
    )


def route_picks(pick, choice, top_count):
    tokens = pick.shape[1]
    routed = tokens * top_count
    token = lax.broadcasted_iota(jnp.int32, (tokens, routed), 0)
    column = lax.broadcasted_iota(jnp.int32, (tokens, routed), 1)
    wide = (column // top_count == token).astype(F32).astype(BF)
    mine = jnp.dot(pick.astype(BF), wide, preferred_element_type=F32)
    which = (lax.broadcasted_iota(jnp.int32, (pick.shape[0], routed), 1) % top_count).astype(F32)
    return jnp.where(which == choice, mine, 0.0)


def pack(peers, steps, extra, *refs):
    sources, refs, count = refs[:4], refs[4 + extra :], len(steps)
    raw_ref, out_refs, held, sems = refs[0], refs[1 : 1 + count], refs[1 + count : -1], refs[-1]
    copies = [
        pltpu.make_async_copy(source, target, sems.at[index])
        for index, (source, target) in enumerate(zip(sources, held))
    ]
    for copy in copies:
        copy.start()
    for copy in copies[:3]:
        copy.wait()
    routes_ref, gates_ref, grad_ref, hidden_ref = held
    hits, place = routing(routes_ref[...], peers, steps)
    gate = gate_of(hits, gates_ref[...])
    choice = choice_of(hits)
    tokens = grad_ref.shape[0]
    wide, quarter = grad_ref.shape[1] // 4, hidden_ref.shape[1] // 4
    low = low_rows(count * ROWS, tokens)
    low_units = low_rows(count * ROWS, quarter)
    last = grad_ref[:, COLS * wide :]
    taken = []
    for block in range(COLS):
        pick = picks(place, block)
        both = jnp.concatenate(
            [jnp.where(low, pick, 0.0).astype(BF), jnp.where(low, 0.0, pick).astype(BF)], axis=1
        )
        columns = slice(block * wide, (block + 1) * wide)
        source = jnp.concatenate([grad_ref[:, columns], last], axis=0)
        packed = jnp.dot(both, source, preferred_element_type=F32).astype(BF)
        for step in range(count):
            out_refs[step][:, columns] = packed[step * ROWS : (step + 1) * ROWS, :]
        take = route_picks(pick, spread(choice, pick), routes_ref.shape[0]).astype(BF)
        taken.append((take, spread(gate, pick)))
    copies[3].wait()
    rows = count * ROWS
    first = jnp.dot(taken[0][0], hidden_ref[:, : COLS * quarter], preferred_element_type=F32)
    rest = jnp.dot(
        jnp.concatenate([take for take, _ in taken], axis=0),
        hidden_ref[:, COLS * quarter :],
        preferred_element_type=F32,
    )
    for block, (_, weight) in enumerate(taken):
        columns = slice(block * quarter, (block + 1) * quarter)
        raw = jnp.where(low_units, first[:, columns], rest[block * rows : (block + 1) * rows, :])
        raw_ref[:, columns] = raw.astype(BF)
        scaled = (weight * raw).astype(BF)
        columns = slice(COLS * wide + block * quarter, COLS * wide + (block + 1) * quarter)
        for step in range(count):
            out_refs[step][:, columns] = scaled[step * ROWS : (step + 1) * ROWS, :]


def maps(peers, routes_ref, gates_ref, weight_ref, block_ref, low_ref, pick_ref, side_ref):
    hits, place = routing(routes_ref[...], peers, range(peers))
    gate, choice = gate_of(hits, gates_ref[...]), choice_of(hits)
    low = low_rows(peers * ROWS, low_ref.shape[0])
    side_ref[...] = jnp.zeros_like(side_ref)
    for block in range(COLS):
        pick = picks(place, block)
        chosen = spread(choice, pick)
        if block == 0:
            take = route_picks(pick, chosen, routes_ref.shape[0])
            low_ref[...] = jnp.where(low, take, 0.0).T.astype(BF)
        pick_ref[block] = pick
        side_ref[:, block : block + 1] = spread(gate, pick)
        side_ref[:, COLS + block : COLS + block + 1] = chosen


def last_quarter(peers, block):
    rows = peers * ROWS
    to = lax.broadcasted_iota(jnp.int32, (rows, rows), 0)
    at = lax.broadcasted_iota(jnp.int32, (rows, rows), 1)
    inside = at % ROWS
    wanted = at - MOST + EXTRA * block
    return ((inside >= MOST) & (to == wanted)).astype(F32).astype(BF)


def block_of(step, peers):
    return pl.ds(pl.multiple_of(partner(lax.axis_index("expert"), step, peers) * ROWS, ROWS), ROWS)


def stack(refs, columns):
    return jnp.concatenate([ref[:, columns] for ref in refs], axis=0)


def unpack_last(peers, parts):
    moves = jnp.concatenate([last_quarter(peers, block) for block in range(COLS)], axis=1)
    return jnp.dot(moves, jnp.concatenate(parts, axis=0), preferred_element_type=F32).astype(BF)


def unit_grads(steps, peers, *refs):
    count, base, extra = len(steps), 0, 1
    in_refs, own_ref, other_ref = refs[:count], refs[count], refs[count + 1]
    refs = refs[count + 2 + extra :]
    here = slice(base * ROWS, (base + count) * ROWS)
    swap_ref, keep_ref = refs[0].at[here], refs[1].at[here]
    out_refs = refs[2:]
    half_units, width = own_ref.shape[1], own_ref.shape[2]
    quarter, wide = half_units // 2, width // 4
    rows = count * ROWS
    first_core = lax.axis_index("dp") == 0
    parts = []
    for block in range(COLS):
        part = stack(in_refs, slice(block * wide, (block + 1) * wide))
        swap_ref[:, block * wide : (block + 1) * wide] = part
        parts.append(part)
    swap_ref[:, COLS * wide : 4 * wide] = unpack_last(count, parts)
    left = swap_ref[:, : 4 * wide]
    across = (((1,), (1,)), ((), ()))
    halves = [
        lax.dot_general(ref[0], left, across, preferred_element_type=F32).T
        for ref in (own_ref, other_ref)
    ]
    low_half = jnp.where(first_core, halves[0], halves[1])
    high_half = jnp.where(first_core, halves[1], halves[0])
    units = [low_half[:, :quarter], low_half[:, quarter:], high_half[:, :quarter]]
    last = high_half[:, quarter:].astype(BF)
    low = low_rows(rows, quarter)
    for block in range(COLS):
        moved = lax.dot_general(
            last_quarter(count, block), last, DOWN, preferred_element_type=F32
        )
        packed = jnp.where(low, units[block], moved).astype(BF)
        for index, step in enumerate(steps):
            out_refs[0][block_of(step, peers), block * quarter : (block + 1) * quarter] = packed[
                index * ROWS : (index + 1) * ROWS, :
            ]
    start = COLS * wide
    parts = [
        stack(in_refs, slice(start + b * quarter, start + (b + 1) * quarter)) for b in range(COLS)
    ]
    scaled = [jnp.where(low, part.astype(F32), 0.0) for part in parts]
    scaled.append(unpack_last(count, parts).astype(F32))
    for place in range(2):
        one, two = scaled[place], scaled[place + 2]
        keep_ref[:, place * quarter : (place + 1) * quarter] = jnp.where(
            first_core, one, two
        ).astype(BF)
        swap_ref[:, width + place * quarter : width + (place + 1) * quarter] = jnp.where(
            first_core, two, one
        ).astype(BF)


def weight_grad(strip, keep_ref, own_ref, other_ref, out_ref, done_ref, held, sems):
    done_ref[...] = jnp.zeros_like(done_ref)
    width = out_ref.shape[2]
    half = out_ref.shape[1]
    left = jnp.concatenate([keep_ref[...], other_ref[:, width : width + half]], axis=0).T
    copies = []
    for index in range(width // strip):
        columns = slice(index * strip, (index + 1) * strip)
        right = jnp.concatenate([own_ref[:, columns], other_ref[:, columns]], axis=0)
        held[index] = jnp.dot(left, right, preferred_element_type=F32).astype(BF)
        copy = pltpu.make_async_copy(held.at[index], out_ref.at[0, :, columns], sems.at[index])
        copy.start()
        copies.append(copy)
    for copy in copies:
        copy.wait()


def finish(peers, packs, pieces, low_ref, pick_ref, side_ref, *refs):
    raw_refs, refs = refs[: len(packs)], refs[len(packs) :]
    found = {step: (ref, at) for ref, pack in zip(raw_refs, packs) for at, step in enumerate(pack)}
    back_ref, (hidden_ref, gate_ref, held, sems) = refs[0], refs[2:]
    top_count = gate_ref.shape[0]
    routed, units = hidden_ref.shape
    quarter = units // 4
    backs, sent = [], []
    for block in range(COLS):
        columns = slice(block * quarter, (block + 1) * quarter)
        back = jnp.concatenate(
            [back_ref[block_of(step, peers), columns] for step in range(peers)], axis=0
        ).astype(F32)
        backs.append(back)
        sent.append((side_ref[:, block : block + 1] * back).astype(BF))
    full = jnp.concatenate([*sent, unpack_last(peers, sent)], axis=1)
    size = routed // pieces
    copies = []
    for piece in range(pieces):
        at = slice(piece * size, (piece + 1) * size)
        held[at] = jnp.dot(low_ref[at, :], full, preferred_element_type=F32).astype(BF)
        copy = pltpu.make_async_copy(held.at[at], hidden_ref.at[at], sems.at[piece])
        copy.start()
        copies.append(copy)
    total = jnp.zeros(gate_ref.shape, F32)
    for block, back in enumerate(backs):
        columns = slice(block * quarter, (block + 1) * quarter)
        raws = jnp.concatenate(
            [
                found[step][0][found[step][1] * ROWS : (found[step][1] + 1) * ROWS, columns]
                for step in range(peers)
            ],
            axis=0,
        )
        value = jnp.sum(raws.astype(F32) * back, axis=1, keepdims=True)
        chosen = side_ref[:, COLS + block : COLS + block + 1]
        weighted = pick_ref[block] * value
        lines = [
            jnp.sum(jnp.where(chosen == float(k), weighted, 0.0), axis=0, keepdims=True)
            for k in range(top_count)
        ]
        total = total + jnp.concatenate(lines, axis=0)
    gate_ref[...] = total
    for copy in copies:
        copy.wait()


def local(out_grad, hidden, routes, gates, w_down):
    tokens, top_count = routes.shape
    units = hidden.shape[2]
    width = out_grad.shape[1]
    half = w_down.shape[1]
    routed = tokens * top_count
    peers = lax.axis_size("expert")
    rows = peers * ROWS
    routes_t, gates_t = routes.T, gates.T
    shape = jax.ShapeDtypeStruct
    room = 20 if peers <= 8 else 60
    half_way = peers // 2
    order = [half_way, *range(1, half_way), *range(half_way + 1, peers)]
    packs = [list(range(peers))]

    def across(array, step, back=False):
        pairs = [(i, partner(i, step, peers)) for i in range(peers)]
        return lax.ppermute(array, "expert", [(b, a) for a, b in pairs] if back else pairs)

    def swap(array):
        return lax.ppermute(array, "dp", [(0, 1), (1, 0)])

    w_other = swap(w_down)
    raws, received = [], {-1: w_other}
    for batch in packs:
        after = list(raws)
        count = len(batch)
        raw, *sent = pl.pallas_call(
            functools.partial(pack, peers, batch, len(raws)),
            out_shape=[shape((count * ROWS, COLS * units // 4), BF)]
            + [shape((ROWS, COLS * (units + width) // 4), BF)] * count,
            in_specs=[pl.BlockSpec(memory_space=pltpu.HBM)] * 4 + [anywhere()] * len(raws),
            out_specs=[vmem()] * (count + 1),
            scratch_shapes=[
                pltpu.VMEM((top_count, tokens), jnp.int32),
                pltpu.VMEM((top_count, tokens), F32),
                pltpu.VMEM((tokens, width), BF),
                pltpu.VMEM((routed, units), BF),
                pltpu.SemaphoreType.DMA((4,)),
            ],
            compiler_params=params(56 if peers <= 8 else 60),
            name="pack",
            cost_estimate=FREE,
        )(routes_t, gates_t, out_grad, hidden.reshape(routed, units), *after)
        raws.append(raw)
        received[0] = sent[0]
        chains = {step: -1 for step in range(half_way + 1, peers)}
        for step in order:
            array = sent[step]
            if step in chains:
                array = lax.optimization_barrier((array, received[chains[step]]))[0]
            received[step] = across(array, step)
    low_map, pick_map, side = pl.pallas_call(
        functools.partial(maps, peers),
        out_shape=[
            shape((routed, rows), BF),
            shape((COLS, rows, tokens), F32),
            shape((rows, 128), F32),
        ],
        in_specs=[vmem()] * 4,
        out_specs=[vmem()] * 3,
        compiler_params=params(room),
        name="maps",
        cost_estimate=FREE,
    )(routes_t, gates_t, w_down, received[0])
    steps = [*order, 0]
    own, keep, back = pl.pallas_call(
        functools.partial(unit_grads, steps, peers),
        out_shape=[
            shape((rows, width + half), BF),
            shape((rows, half), BF),
            shape((rows, COLS * units // 4), BF),
        ],
        in_specs=[vmem()] * (peers + 2) + [anywhere()],
        out_specs=[vmem()] * 3,
        compiler_params=params(room),
        name="unit_grads",
        cost_estimate=FREE,
    )(*[received[step] for step in steps], w_down, w_other, pick_map)
    other = swap(own)
    back = lax.all_to_all(back, "expert", split_axis=0, concat_axis=0, tiled=True)
    strip = 512 if width % 512 == 0 else width
    grad_down, done = pl.pallas_call(
        functools.partial(weight_grad, strip),
        out_shape=[shape((1, half, width), BF), shape((8, 128), F32)],
        in_specs=[vmem()] * 3,
        out_specs=[anywhere(), vmem()],
        scratch_shapes=[
            pltpu.VMEM((width // strip, half, strip), BF),
            pltpu.SemaphoreType.DMA((width // strip,)),
        ],
        compiler_params=params(room),
        name="weight_grad",
    )(keep, own, other)
    pieces = 4
    grad_hidden, grad_gates_t = pl.pallas_call(
        functools.partial(finish, peers, packs, pieces),
        out_shape=[shape((routed, units), BF), shape((top_count, tokens), F32)],
        in_specs=[vmem()] * (4 + len(packs)) + [anywhere()],
        out_specs=[anywhere(), vmem()],
        scratch_shapes=[pltpu.VMEM((routed, units), BF), pltpu.SemaphoreType.DMA((pieces,))],
        compiler_params=params(room),
        name="finish",
    )(low_map, pick_map, side, *raws, back, done)
    return grad_down, grad_hidden.reshape(tokens, top_count, units), grad_gates_t.T


def solution(mesh):
    in_specs = (
        P(("groups", "expert", "dp"), None),
        P(("groups", "expert", "dp"), None, None),
        P(("groups", "expert", "dp"), None),
        P(("groups", "expert", "dp"), None),
        P("expert", "dp", None),
    )
    out_specs = (
        P(("groups", "expert"), "dp", None),
        P(("groups", "expert", "dp"), None, None),
        P(("groups", "expert", "dp"), None),
    )
    return jax.shard_map(local, mesh=mesh, in_specs=in_specs, out_specs=out_specs, check_vma=False)
```

```python
import functools

import jax
import jax.numpy as jnp
from jax import lax
from jax.experimental import pallas as pl
from jax.experimental.pallas import tpu as pltpu
from jax.sharding import PartitionSpec as P

MOST = 12
ROWS = 16
COLS = 3
EXTRA = ROWS - MOST
BF = jnp.bfloat16
F32 = jnp.float32
MIB = 1 << 20
DOWN = (((0,), (0,)), ((), ()))


FREE = pl.CostEstimate(flops=0, bytes_accessed=0, transcendentals=0)


def params(mib=20, **kw):
    return pltpu.CompilerParams(vmem_limit_bytes=mib * MIB, **kw)


def vmem():
    return pl.BlockSpec(memory_space=pltpu.VMEM)


def anywhere():
    return pl.BlockSpec(memory_space=pl.ANY)


def partner(index, step, peers):
    if peers & (peers - 1) == 0:
        return index ^ step
    return lax.rem(index + step, peers) if isinstance(index, jax.Array) else (index + step) % peers


def routing(routes_t, peers, steps):
    me = lax.axis_index("expert")
    tokens = routes_t.shape[1]
    hits = [routes_t == partner(me, step, peers) for step in steps]
    member = jnp.concatenate(
        [jnp.max(hit.astype(F32), axis=0, keepdims=True) for hit in hits], axis=0
    )
    earlier = lax.broadcasted_iota(jnp.int32, (tokens, tokens), 0) < lax.broadcasted_iota(
        jnp.int32, (tokens, tokens), 1
    )
    before = jnp.dot(member.astype(BF), earlier.astype(F32).astype(BF), preferred_element_type=F32)
    return hits, jnp.where(member > 0, before, -1.0)


def picks(place, block):
    tokens = place.shape[1]
    row = lax.broadcasted_iota(jnp.int32, (ROWS, tokens), 0)
    wanted = jnp.where(row < MOST, row, row - MOST + EXTRA * block).astype(F32)
    return jnp.concatenate(
        [(place[step : step + 1, :] == wanted).astype(F32) for step in range(place.shape[0])], axis=0
    )


def low_rows(rows, width):
    inside = lax.rem(lax.broadcasted_iota(jnp.int32, (rows, 1), 0), ROWS)
    return jnp.broadcast_to(inside, (rows, width)) < MOST


def gate_of(hits, gates_t):
    return jnp.concatenate(
        [jnp.sum(jnp.where(hit, gates_t, 0.0), axis=0, keepdims=True) for hit in hits], axis=0
    )


def choice_of(hits):
    return jnp.concatenate(
        [
            jnp.sum(
                jnp.where(hit, lax.broadcasted_iota(jnp.int32, hit.shape, 0).astype(F32), 0.0),
                axis=0,
                keepdims=True,
            )
            for hit in hits
        ],
        axis=0,
    )


def spread(table, pick):
    return jnp.concatenate(
        [
            jnp.sum(
                pick[step * ROWS : (step + 1) * ROWS, :] * table[step : step + 1, :],
                axis=1,
                keepdims=True,
            )
            for step in range(table.shape[0])
        ],
        axis=0,
    )


def route_picks(pick, choice, top_count):
    tokens = pick.shape[1]
    routed = tokens * top_count
    column = lax.broadcasted_iota(jnp.int32, (1, routed), 1)
    of_token = jnp.broadcast_to(lax.div(column, top_count), (tokens, routed))
    token = lax.broadcasted_iota(jnp.int32, (tokens, routed), 0)
    wide = (of_token == token).astype(F32).astype(BF)
    mine = jnp.dot(pick.astype(BF), wide, preferred_element_type=F32)
    which = lax.rem(column, top_count).astype(F32)
    return jnp.where(which == choice, mine, 0.0)


def pack(peers, steps, extra, *refs):
    sources, refs, count = refs[:4], refs[4 + extra :], len(steps)
    raw_ref, out_refs, held, sems = refs[0], refs[1 : 1 + count], refs[1 + count : -1], refs[-1]
    copies = [
        pltpu.make_async_copy(source, target, sems.at[index])
        for index, (source, target) in enumerate(zip(sources, held))
    ]
    for copy in copies:
        copy.start()
    for copy in copies[:3]:
        copy.wait()
    routes_ref, gates_ref, grad_ref, hidden_ref = held
    hits, place = routing(routes_ref[...], peers, steps)
    gate = gate_of(hits, gates_ref[...])
    choice = choice_of(hits)
    tokens = grad_ref.shape[0]
    wide, quarter = grad_ref.shape[1] // 4, hidden_ref.shape[1] // 4
    low = low_rows(count * ROWS, tokens)
    low_units = low_rows(count * ROWS, quarter)
    last = grad_ref[:, COLS * wide :]
    taken = []
    for block in range(COLS):
        pick = picks(place, block)
        both = jnp.concatenate(
            [jnp.where(low, pick, 0.0).astype(BF), jnp.where(low, 0.0, pick).astype(BF)], axis=1
        )
        columns = slice(block * wide, (block + 1) * wide)
        source = jnp.concatenate([grad_ref[:, columns], last], axis=0)
        packed = jnp.dot(both, source, preferred_element_type=F32).astype(BF)
        for step in range(count):
            out_refs[step][:, columns] = packed[step * ROWS : (step + 1) * ROWS, :]
        take = route_picks(pick, spread(choice, pick), routes_ref.shape[0]).astype(BF)
        taken.append((take, spread(gate, pick)))
    copies[3].wait()
    rows = count * ROWS
    first = jnp.dot(taken[0][0], hidden_ref[:, : COLS * quarter], preferred_element_type=F32)
    rest = jnp.dot(
        jnp.concatenate([take for take, _ in taken], axis=0),
        hidden_ref[:, COLS * quarter :],
        preferred_element_type=F32,
    )
    for block, (_, weight) in enumerate(taken):
        columns = slice(block * quarter, (block + 1) * quarter)
        raw = jnp.where(low_units, first[:, columns], rest[block * rows : (block + 1) * rows, :])
        raw_ref[:, columns] = raw.astype(BF)
        scaled = (weight * raw).astype(BF)
        columns = slice(COLS * wide + block * quarter, COLS * wide + (block + 1) * quarter)
        for step in range(count):
            out_refs[step][:, columns] = scaled[step * ROWS : (step + 1) * ROWS, :]


def maps(peers, routes_ref, gates_ref, weight_ref, block_ref, low_ref, pick_ref, side_ref):
    hits, place = routing(routes_ref[...], peers, range(peers))
    gate, choice = gate_of(hits, gates_ref[...]), choice_of(hits)
    low = low_rows(peers * ROWS, low_ref.shape[0])
    side_ref[...] = jnp.zeros_like(side_ref)
    for block in range(COLS):
        pick = picks(place, block)
        chosen = spread(choice, pick)
        if block == 0:
            take = route_picks(pick, chosen, routes_ref.shape[0])
            low_ref[...] = jnp.where(low, take, 0.0).T.astype(BF)
        pick_ref[block] = pick
        side_ref[:, block : block + 1] = spread(gate, pick)
        side_ref[:, COLS + block : COLS + block + 1] = chosen


def last_quarter(peers, block):
    rows = peers * ROWS
    to = lax.broadcasted_iota(jnp.int32, (rows, rows), 0)
    at = lax.broadcasted_iota(jnp.int32, (1, rows), 1)
    wanted = jnp.where(lax.rem(at, ROWS) >= MOST, at - MOST + EXTRA * block, -1)
    return (to == jnp.broadcast_to(wanted, (rows, rows))).astype(F32).astype(BF)


def block_of(step, peers):
    return pl.ds(pl.multiple_of(partner(lax.axis_index("expert"), step, peers) * ROWS, ROWS), ROWS)


def stack(refs, columns):
    return jnp.concatenate([ref[:, columns] for ref in refs], axis=0)


def unpack_last(peers, parts):
    moves = jnp.concatenate([last_quarter(peers, block) for block in range(COLS)], axis=1)
    return jnp.dot(moves, jnp.concatenate(parts, axis=0), preferred_element_type=F32).astype(BF)


def unit_grads(steps, peers, *refs):
    count, base, extra = len(steps), 0, 1
    in_refs, own_ref, other_ref = refs[:count], refs[count], refs[count + 1]
    refs = refs[count + 2 + extra :]
    here = slice(base * ROWS, (base + count) * ROWS)
    swap_ref, keep_ref = refs[0].at[here], refs[1].at[here]
    out_refs = refs[2:]
    half_units, width = own_ref.shape[1], own_ref.shape[2]
    quarter, wide = half_units // 2, width // 4
    rows = count * ROWS
    first_core = lax.axis_index("dp") == 0
    parts = []
    for block in range(COLS):
        part = stack(in_refs, slice(block * wide, (block + 1) * wide))
        swap_ref[:, block * wide : (block + 1) * wide] = part
        parts.append(part)
    swap_ref[:, COLS * wide : 4 * wide] = unpack_last(count, parts)
    left = swap_ref[:, : 4 * wide]
    across = (((1,), (1,)), ((), ()))
    halves = [
        lax.dot_general(ref[0], left, across, preferred_element_type=F32).T
        for ref in (own_ref, other_ref)
    ]
    low_half = jnp.where(first_core, halves[0], halves[1])
    high_half = jnp.where(first_core, halves[1], halves[0])
    units = [low_half[:, :quarter], low_half[:, quarter:], high_half[:, :quarter]]
    last = high_half[:, quarter:].astype(BF)
    low = low_rows(rows, quarter)
    for block in range(COLS):
        moved = lax.dot_general(
            last_quarter(count, block), last, DOWN, preferred_element_type=F32
        )
        packed = jnp.where(low, units[block], moved).astype(BF)
        for index, step in enumerate(steps):
            out_refs[0][block_of(step, peers), block * quarter : (block + 1) * quarter] = packed[
                index * ROWS : (index + 1) * ROWS, :
            ]
    start = COLS * wide
    parts = [
        stack(in_refs, slice(start + b * quarter, start + (b + 1) * quarter)) for b in range(COLS)
    ]
    scaled = [jnp.where(low, part.astype(F32), 0.0) for part in parts]
    scaled.append(unpack_last(count, parts).astype(F32))
    for place in range(2):
        one, two = scaled[place], scaled[place + 2]
        keep_ref[:, place * quarter : (place + 1) * quarter] = jnp.where(
            first_core, one, two
        ).astype(BF)
        swap_ref[:, width + place * quarter : width + (place + 1) * quarter] = jnp.where(
            first_core, two, one
        ).astype(BF)


def weight_grad(strip, keep_ref, own_ref, other_ref, out_ref, done_ref, held, sems):
    done_ref[...] = jnp.zeros_like(done_ref)
    width = out_ref.shape[2]
    half = out_ref.shape[1]
    left = jnp.concatenate([keep_ref[...], other_ref[:, width : width + half]], axis=0).T
    copies = []
    for index in range(width // strip):
        columns = slice(index * strip, (index + 1) * strip)
        right = jnp.concatenate([own_ref[:, columns], other_ref[:, columns]], axis=0)
        held[index] = jnp.dot(left, right, preferred_element_type=F32).astype(BF)
        copy = pltpu.make_async_copy(held.at[index], out_ref.at[0, :, columns], sems.at[index])
        copy.start()
        copies.append(copy)
    for copy in copies:
        copy.wait()


def finish(peers, packs, pieces, low_ref, pick_ref, side_ref, *refs):
    raw_refs, refs = refs[: len(packs)], refs[len(packs) :]
    found = {step: (ref, at) for ref, pack in zip(raw_refs, packs) for at, step in enumerate(pack)}
    back_ref, (hidden_ref, gate_ref, held, sems) = refs[0], refs[2:]
    top_count = gate_ref.shape[0]
    routed, units = hidden_ref.shape
    quarter = units // 4
    backs, sent = [], []
    for block in range(COLS):
        columns = slice(block * quarter, (block + 1) * quarter)
        back = jnp.concatenate(
            [back_ref[block_of(step, peers), columns] for step in range(peers)], axis=0
        ).astype(F32)
        backs.append(back)
        sent.append((side_ref[:, block : block + 1] * back).astype(BF))
    full = jnp.concatenate([*sent, unpack_last(peers, sent)], axis=1)
    size = routed // pieces
    copies = []
    for piece in range(pieces):
        at = slice(piece * size, (piece + 1) * size)
        held[at] = jnp.dot(low_ref[at, :], full, preferred_element_type=F32).astype(BF)
        copy = pltpu.make_async_copy(held.at[at], hidden_ref.at[at], sems.at[piece])
        copy.start()
        copies.append(copy)
    total = jnp.zeros(gate_ref.shape, F32)
    for block, back in enumerate(backs):
        columns = slice(block * quarter, (block + 1) * quarter)
        raws = jnp.concatenate(
            [
                found[step][0][found[step][1] * ROWS : (found[step][1] + 1) * ROWS, columns]
                for step in range(peers)
            ],
            axis=0,
        )
        value = jnp.sum(raws.astype(F32) * back, axis=1, keepdims=True)
        chosen = side_ref[:, COLS + block : COLS + block + 1]
        weighted = pick_ref[block] * value
        lines = [
            jnp.sum(jnp.where(chosen == float(k), weighted, 0.0), axis=0, keepdims=True)
            for k in range(top_count)
        ]
        total = total + jnp.concatenate(lines, axis=0)
    gate_ref[...] = total
    for copy in copies:
        copy.wait()


def local(out_grad, hidden, routes, gates, w_down):
    tokens, top_count = routes.shape
    units = hidden.shape[2]
    width = out_grad.shape[1]
    half = w_down.shape[1]
    routed = tokens * top_count
    peers = lax.axis_size("expert")
    rows = peers * ROWS
    routes_t, gates_t = routes.T, gates.T
    shape = jax.ShapeDtypeStruct
    room = 20 if peers <= 8 else 60
    half_way = peers // 2
    order = [half_way, *range(1, half_way), *range(half_way + 1, peers)]
    packs = [list(range(peers))]

    def across(array, step, back=False):
        pairs = [(i, partner(i, step, peers)) for i in range(peers)]
        return lax.ppermute(array, "expert", [(b, a) for a, b in pairs] if back else pairs)

    def swap(array):
        return lax.ppermute(array, "dp", [(0, 1), (1, 0)])

    w_other = swap(w_down)
    raws, received = [], {-1: w_other}
    for batch in packs:
        after = list(raws)
        count = len(batch)
        raw, *sent = pl.pallas_call(
            functools.partial(pack, peers, batch, len(raws)),
            out_shape=[shape((count * ROWS, COLS * units // 4), BF)]
            + [shape((ROWS, COLS * (units + width) // 4), BF)] * count,
            in_specs=[pl.BlockSpec(memory_space=pltpu.HBM)] * 4 + [anywhere()] * len(raws),
            out_specs=[vmem()] * (count + 1),
            scratch_shapes=[
                pltpu.VMEM((top_count, tokens), jnp.int32),
                pltpu.VMEM((top_count, tokens), F32),
                pltpu.VMEM((tokens, width), BF),
                pltpu.VMEM((routed, units), BF),
                pltpu.SemaphoreType.DMA((4,)),
            ],
            compiler_params=params(56 if peers <= 8 else 60),
            name="pack",
            cost_estimate=FREE,
        )(routes_t, gates_t, out_grad, hidden.reshape(routed, units), *after)
        raws.append(raw)
        received[0] = sent[0]
        chains = {step: -1 for step in range(half_way + 1, peers)}
        for step in order:
            array = sent[step]
            if step in chains:
                array = lax.optimization_barrier((array, received[chains[step]]))[0]
            received[step] = across(array, step)
    low_map, pick_map, side = pl.pallas_call(
        functools.partial(maps, peers),
        out_shape=[
            shape((routed, rows), BF),
            shape((COLS, rows, tokens), F32),
            shape((rows, 128), F32),
        ],
        in_specs=[vmem()] * 4,
        out_specs=[vmem()] * 3,
        compiler_params=params(room),
        name="maps",
        cost_estimate=FREE,
    )(routes_t, gates_t, w_down, received[0])
    steps = [*order, 0]
    own, keep, back = pl.pallas_call(
        functools.partial(unit_grads, steps, peers),
        out_shape=[
            shape((rows, width + half), BF),
            shape((rows, half), BF),
            shape((rows, COLS * units // 4), BF),
        ],
        in_specs=[vmem()] * (peers + 2) + [anywhere()],
        out_specs=[vmem()] * 3,
        compiler_params=params(room),
        name="unit_grads",
        cost_estimate=FREE,
    )(*[received[step] for step in steps], w_down, w_other, pick_map)
    other = swap(own)
    back = lax.all_to_all(back, "expert", split_axis=0, concat_axis=0, tiled=True)
    strip = 512 if width % 512 == 0 else width
    grad_down, done = pl.pallas_call(
        functools.partial(weight_grad, strip),
        out_shape=[shape((1, half, width), BF), shape((8, 128), F32)],
        in_specs=[vmem()] * 3,
        out_specs=[anywhere(), vmem()],
        scratch_shapes=[
            pltpu.VMEM((width // strip, half, strip), BF),
            pltpu.SemaphoreType.DMA((width // strip,)),
        ],
        compiler_params=params(room),
        name="weight_grad",
    )(keep, own, other)
    pieces = 4
    grad_hidden, grad_gates_t = pl.pallas_call(
        functools.partial(finish, peers, packs, pieces),
        out_shape=[shape((routed, units), BF), shape((top_count, tokens), F32)],
        in_specs=[vmem()] * (4 + len(packs)) + [anywhere()],
        out_specs=[anywhere(), vmem()],
        scratch_shapes=[pltpu.VMEM((routed, units), BF), pltpu.SemaphoreType.DMA((pieces,))],
        compiler_params=params(room),
        name="finish",
    )(low_map, pick_map, side, *raws, back, done)
    return grad_down, grad_hidden.reshape(tokens, top_count, units), grad_gates_t.T


def solution(mesh):
    in_specs = (
        P(("groups", "expert", "dp"), None),
        P(("groups", "expert", "dp"), None, None),
        P(("groups", "expert", "dp"), None),
        P(("groups", "expert", "dp"), None),
        P("expert", "dp", None),
    )
    out_specs = (
        P(("groups", "expert"), "dp", None),
        P(("groups", "expert", "dp"), None, None),
        P(("groups", "expert", "dp"), None),
    )
    return jax.shard_map(local, mesh=mesh, in_specs=in_specs, out_specs=out_specs, check_vma=False)
```

```python
import functools

import jax
import jax.numpy as jnp
from jax import lax
from jax.experimental import pallas as pl
from jax.experimental.pallas import tpu as pltpu
from jax.sharding import PartitionSpec as P

MOST = 12
ROWS = 16
COLS = 3
EXTRA = ROWS - MOST
BF = jnp.bfloat16
F32 = jnp.float32
MIB = 1 << 20
DOWN = (((0,), (0,)), ((), ()))


FREE = pl.CostEstimate(flops=0, bytes_accessed=0, transcendentals=0)


def params(mib=20, **kw):
    return pltpu.CompilerParams(vmem_limit_bytes=mib * MIB, **kw)


def vmem():
    return pl.BlockSpec(memory_space=pltpu.VMEM)


def anywhere():
    return pl.BlockSpec(memory_space=pl.ANY)


def partner(index, step, peers):
    if peers & (peers - 1) == 0:
        return index ^ step
    return lax.rem(index + step, peers) if isinstance(index, jax.Array) else (index + step) % peers


def routing(routes_t, peers, steps):
    me = lax.axis_index("expert")
    tokens = routes_t.shape[1]
    hits = [routes_t == partner(me, step, peers) for step in steps]
    member = jnp.concatenate(
        [jnp.max(hit.astype(F32), axis=0, keepdims=True) for hit in hits], axis=0
    )
    earlier = lax.broadcasted_iota(jnp.int32, (tokens, tokens), 0) < lax.broadcasted_iota(
        jnp.int32, (tokens, tokens), 1
    )
    before = jnp.dot(member.astype(BF), earlier.astype(F32).astype(BF), preferred_element_type=F32)
    return hits, jnp.where(member > 0, before, -1.0)


def picks(place, block):
    tokens = place.shape[1]
    row = lax.broadcasted_iota(jnp.int32, (ROWS, tokens), 0)
    wanted = jnp.where(row < MOST, row, row - MOST + EXTRA * block).astype(F32)
    return jnp.concatenate(
        [(place[step : step + 1, :] == wanted).astype(F32) for step in range(place.shape[0])], axis=0
    )


def low_rows(rows, width):
    inside = lax.rem(lax.broadcasted_iota(jnp.int32, (rows, 1), 0), ROWS)
    return jnp.broadcast_to(inside, (rows, width)) < MOST


def gate_of(hits, gates_t):
    return jnp.concatenate(
        [jnp.sum(jnp.where(hit, gates_t, 0.0), axis=0, keepdims=True) for hit in hits], axis=0
    )


def choice_of(hits):
    return jnp.concatenate(
        [
            jnp.sum(
                jnp.where(hit, lax.broadcasted_iota(jnp.int32, hit.shape, 0).astype(F32), 0.0),
                axis=0,
                keepdims=True,
            )
            for hit in hits
        ],
        axis=0,
    )


def spread(table, pick):
    return jnp.concatenate(
        [
            jnp.sum(
                pick[step * ROWS : (step + 1) * ROWS, :] * table[step : step + 1, :],
                axis=1,
                keepdims=True,
            )
            for step in range(table.shape[0])
        ],
        axis=0,
    )


def route_picks(pick, choice, top_count):
    tokens = pick.shape[1]
    routed = tokens * top_count
    column = lax.broadcasted_iota(jnp.int32, (1, routed), 1)
    of_token = jnp.broadcast_to(lax.div(column, top_count), (tokens, routed))
    token = lax.broadcasted_iota(jnp.int32, (tokens, routed), 0)
    wide = (of_token == token).astype(F32).astype(BF)
    mine = jnp.dot(pick.astype(BF), wide, preferred_element_type=F32)
    which = lax.rem(column, top_count).astype(F32)
    return jnp.where(which == choice, mine, 0.0)


def pack(peers, steps, extra, *refs):
    sources, refs, count = refs[:4], refs[4 + extra :], len(steps)
    raw_ref, out_refs, held, sems = refs[0], refs[1 : 1 + count], refs[1 + count : -1], refs[-1]
    copies = [
        pltpu.make_async_copy(source, target, sems.at[index])
        for index, (source, target) in enumerate(zip(sources, held))
    ]
    for copy in copies:
        copy.start()
    for copy in copies[:3]:
        copy.wait()
    routes_ref, gates_ref, grad_ref, hidden_ref = held
    hits, place = routing(routes_ref[...], peers, steps)
    gate = gate_of(hits, gates_ref[...])
    choice = choice_of(hits)
    tokens = grad_ref.shape[0]
    wide, quarter = grad_ref.shape[1] // 4, hidden_ref.shape[1] // 4
    low = low_rows(count * ROWS, tokens)
    low_units = low_rows(count * ROWS, quarter)
    last = grad_ref[:, COLS * wide :]
    taken = []
    for block in range(COLS):
        pick = picks(place, block)
        both = jnp.concatenate(
            [jnp.where(low, pick, 0.0).astype(BF), jnp.where(low, 0.0, pick).astype(BF)], axis=1
        )
        columns = slice(block * wide, (block + 1) * wide)
        source = jnp.concatenate([grad_ref[:, columns], last], axis=0)
        packed = jnp.dot(both, source, preferred_element_type=F32).astype(BF)
        for step in range(count):
            out_refs[step][:, columns] = packed[step * ROWS : (step + 1) * ROWS, :]
        take = route_picks(pick, spread(choice, pick), routes_ref.shape[0]).astype(BF)
        taken.append((take, spread(gate, pick)))
    copies[3].wait()
    rows = count * ROWS
    first = jnp.dot(taken[0][0], hidden_ref[:, : COLS * quarter], preferred_element_type=F32)
    rest = jnp.dot(
        jnp.concatenate([take for take, _ in taken], axis=0),
        hidden_ref[:, COLS * quarter :],
        preferred_element_type=F32,
    )
    for block, (_, weight) in enumerate(taken):
        columns = slice(block * quarter, (block + 1) * quarter)
        raw = jnp.where(low_units, first[:, columns], rest[block * rows : (block + 1) * rows, :])
        raw_ref[:, columns] = raw.astype(BF)
        scaled = (weight * raw).astype(BF)
        columns = slice(COLS * wide + block * quarter, COLS * wide + (block + 1) * quarter)
        for step in range(count):
            out_refs[step][:, columns] = scaled[step * ROWS : (step + 1) * ROWS, :]


def maps(peers, routes_ref, gates_ref, weight_ref, block_ref, low_ref, pick_ref, side_ref):
    hits, place = routing(routes_ref[...], peers, range(peers))
    gate, choice = gate_of(hits, gates_ref[...]), choice_of(hits)
    low = low_rows(peers * ROWS, low_ref.shape[0])
    side_ref[...] = jnp.zeros_like(side_ref)
    for block in range(COLS):
        pick = picks(place, block)
        chosen = spread(choice, pick)
        if block == 0:
            take = route_picks(pick, chosen, routes_ref.shape[0])
            low_ref[...] = jnp.where(low, take, 0.0).T.astype(BF)
        pick_ref[block] = pick
        side_ref[:, block : block + 1] = spread(gate, pick)
        side_ref[:, COLS + block : COLS + block + 1] = chosen


def last_quarter(peers, block):
    rows = peers * ROWS
    to = lax.broadcasted_iota(jnp.int32, (rows, rows), 0)
    at = lax.broadcasted_iota(jnp.int32, (1, rows), 1)
    wanted = jnp.where(lax.rem(at, ROWS) >= MOST, at - MOST + EXTRA * block, -1)
    return (to == jnp.broadcast_to(wanted, (rows, rows))).astype(F32).astype(BF)


def block_of(step, peers):
    return pl.ds(pl.multiple_of(partner(lax.axis_index("expert"), step, peers) * ROWS, ROWS), ROWS)


def stack(refs, columns):
    return jnp.concatenate([ref[:, columns] for ref in refs], axis=0)


def unpack_last(peers, parts):
    moves = jnp.concatenate([last_quarter(peers, block) for block in range(COLS)], axis=1)
    return jnp.dot(moves, jnp.concatenate(parts, axis=0), preferred_element_type=F32).astype(BF)


def unit_grads(steps, peers, *refs):
    count, base, extra = len(steps), 0, 1
    in_refs, own_ref, other_ref = refs[:count], refs[count], refs[count + 1]
    refs = refs[count + 2 + extra :]
    here = slice(base * ROWS, (base + count) * ROWS)
    swap_ref, keep_ref = refs[0].at[here], refs[1].at[here]
    out_refs = refs[2:]
    half_units, width = own_ref.shape[1], own_ref.shape[2]
    quarter, wide = half_units // 2, width // 4
    rows = count * ROWS
    first_core = lax.axis_index("dp") == 0
    parts = []
    for block in range(COLS):
        part = stack(in_refs, slice(block * wide, (block + 1) * wide))
        swap_ref[:, block * wide : (block + 1) * wide] = part
        parts.append(part)
    swap_ref[:, COLS * wide : 4 * wide] = unpack_last(count, parts)
    left = swap_ref[:, : 4 * wide]
    across = (((1,), (1,)), ((), ()))
    halves = [
        lax.dot_general(ref[0], left, across, preferred_element_type=F32).T
        for ref in (own_ref, other_ref)
    ]
    low_half = jnp.where(first_core, halves[0], halves[1])
    high_half = jnp.where(first_core, halves[1], halves[0])
    units = [low_half[:, :quarter], low_half[:, quarter:], high_half[:, :quarter]]
    last = high_half[:, quarter:].astype(BF)
    low = low_rows(rows, quarter)
    for block in range(COLS):
        moved = lax.dot_general(
            last_quarter(count, block), last, DOWN, preferred_element_type=F32
        )
        packed = jnp.where(low, units[block], moved).astype(BF)
        for index, step in enumerate(steps):
            out_refs[0][block_of(step, peers), block * quarter : (block + 1) * quarter] = packed[
                index * ROWS : (index + 1) * ROWS, :
            ]
    start = COLS * wide
    parts = [
        stack(in_refs, slice(start + b * quarter, start + (b + 1) * quarter)) for b in range(COLS)
    ]
    scaled = [jnp.where(low, part.astype(F32), 0.0) for part in parts]
    scaled.append(unpack_last(count, parts).astype(F32))
    for place in range(2):
        one, two = scaled[place], scaled[place + 2]
        keep_ref[:, place * quarter : (place + 1) * quarter] = jnp.where(
            first_core, one, two
        ).astype(BF)
        swap_ref[:, width + place * quarter : width + (place + 1) * quarter] = jnp.where(
            first_core, two, one
        ).astype(BF)


def weight_grad(strip, keep_ref, own_ref, other_ref, out_ref, done_ref, held, sems):
    done_ref[...] = jnp.zeros_like(done_ref)
    width = out_ref.shape[2]
    half = out_ref.shape[1]
    left = jnp.concatenate([keep_ref[...], other_ref[:, width : width + half]], axis=0).T
    copies = []
    for index in range(width // strip):
        columns = slice(index * strip, (index + 1) * strip)
        right = jnp.concatenate([own_ref[:, columns], other_ref[:, columns]], axis=0)
        held[index] = jnp.dot(left, right, preferred_element_type=F32).astype(BF)
        copy = pltpu.make_async_copy(held.at[index], out_ref.at[0, :, columns], sems.at[index])
        copy.start()
        copies.append(copy)
    for copy in copies:
        copy.wait()


def finish(peers, packs, pieces, low_ref, pick_ref, side_ref, *refs):
    raw_refs, refs = refs[: len(packs)], refs[len(packs) :]
    found = {step: (ref, at) for ref, pack in zip(raw_refs, packs) for at, step in enumerate(pack)}
    back_ref, (hidden_ref, gate_ref, held, sems) = refs[0], refs[2:]
    top_count = gate_ref.shape[0]
    routed, units = hidden_ref.shape
    quarter = units // 4
    backs, sent = [], []
    for block in range(COLS):
        columns = slice(block * quarter, (block + 1) * quarter)
        back = jnp.concatenate(
            [back_ref[block_of(step, peers), columns] for step in range(peers)], axis=0
        ).astype(F32)
        backs.append(back)
        sent.append((side_ref[:, block : block + 1] * back).astype(BF))
    full = jnp.concatenate([*sent, unpack_last(peers, sent)], axis=1)
    size = routed // pieces
    copies = []
    for piece in range(pieces):
        at = slice(piece * size, (piece + 1) * size)
        held[at] = jnp.dot(low_ref[at, :], full, preferred_element_type=F32).astype(BF)
        copy = pltpu.make_async_copy(held.at[at], hidden_ref.at[at], sems.at[piece])
        copy.start()
        copies.append(copy)
    total = jnp.zeros(gate_ref.shape, F32)
    for block, back in enumerate(backs):
        columns = slice(block * quarter, (block + 1) * quarter)
        raws = jnp.concatenate(
            [
                found[step][0][found[step][1] * ROWS : (found[step][1] + 1) * ROWS, columns]
                for step in range(peers)
            ],
            axis=0,
        )
        value = jnp.sum(raws.astype(F32) * back, axis=1, keepdims=True)
        chosen = side_ref[:, COLS + block : COLS + block + 1]
        weighted = pick_ref[block] * value
        lines = [
            jnp.sum(jnp.where(chosen == float(k), weighted, 0.0), axis=0, keepdims=True)
            for k in range(top_count)
        ]
        total = total + jnp.concatenate(lines, axis=0)
    gate_ref[...] = total
    for copy in copies:
        copy.wait()


def local(out_grad, hidden, routes, gates, w_down):
    tokens, top_count = routes.shape
    units = hidden.shape[2]
    width = out_grad.shape[1]
    half = w_down.shape[1]
    routed = tokens * top_count
    peers = lax.axis_size("expert")
    rows = peers * ROWS
    routes_t, gates_t = routes.T, gates.T
    shape = jax.ShapeDtypeStruct
    room = 20 if peers <= 8 else 60
    half_way = peers // 2
    order = [half_way, *range(half_way - 1, 0, -1), *range(half_way + 1, peers)]
    packs = [list(range(peers))]

    def across(array, step, back=False):
        pairs = [(i, partner(i, step, peers)) for i in range(peers)]
        return lax.ppermute(array, "expert", [(b, a) for a, b in pairs] if back else pairs)

    def swap(array):
        return lax.ppermute(array, "dp", [(0, 1), (1, 0)])

    w_other = swap(w_down)
    raws, received = [], {-1: w_other}
    for batch in packs:
        after = list(raws)
        count = len(batch)
        raw, *sent = pl.pallas_call(
            functools.partial(pack, peers, batch, len(raws)),
            out_shape=[shape((count * ROWS, COLS * units // 4), BF)]
            + [shape((ROWS, COLS * (units + width) // 4), BF)] * count,
            in_specs=[pl.BlockSpec(memory_space=pltpu.HBM)] * 4 + [anywhere()] * len(raws),
            out_specs=[vmem()] * (count + 1),
            scratch_shapes=[
                pltpu.VMEM((top_count, tokens), jnp.int32),
                pltpu.VMEM((top_count, tokens), F32),
                pltpu.VMEM((tokens, width), BF),
                pltpu.VMEM((routed, units), BF),
                pltpu.SemaphoreType.DMA((4,)),
            ],
            compiler_params=params(56 if peers <= 8 else 60),
            name="pack",
            cost_estimate=FREE,
        )(routes_t, gates_t, out_grad, hidden.reshape(routed, units), *after)
        raws.append(raw)
        received[0] = sent[0]
        chains = {step: -1 for step in range(half_way + 1, peers)}
        for step in order:
            array = sent[step]
            if step in chains:
                array = lax.optimization_barrier((array, received[chains[step]]))[0]
            received[step] = across(array, step)
    low_map, pick_map, side = pl.pallas_call(
        functools.partial(maps, peers),
        out_shape=[
            shape((routed, rows), BF),
            shape((COLS, rows, tokens), F32),
            shape((rows, 128), F32),
        ],
        in_specs=[vmem()] * 4,
        out_specs=[vmem()] * 3,
        compiler_params=params(room),
        name="maps",
        cost_estimate=FREE,
    )(routes_t, gates_t, w_down, received[0])
    steps = [*order, 0]
    own, keep, back = pl.pallas_call(
        functools.partial(unit_grads, steps, peers),
        out_shape=[
            shape((rows, width + half), BF),
            shape((rows, half), BF),
            shape((rows, COLS * units // 4), BF),
        ],
        in_specs=[vmem()] * (peers + 2) + [anywhere()],
        out_specs=[vmem()] * 3,
        compiler_params=params(room),
        name="unit_grads",
        cost_estimate=FREE,
    )(*[received[step] for step in steps], w_down, w_other, pick_map)
    other = swap(own)
    back = lax.all_to_all(back, "expert", split_axis=0, concat_axis=0, tiled=True)
    strip = 512 if width % 512 == 0 else width
    grad_down, done = pl.pallas_call(
        functools.partial(weight_grad, strip),
        out_shape=[shape((1, half, width), BF), shape((8, 128), F32)],
        in_specs=[vmem()] * 3,
        out_specs=[anywhere(), vmem()],
        scratch_shapes=[
            pltpu.VMEM((width // strip, half, strip), BF),
            pltpu.SemaphoreType.DMA((width // strip,)),
        ],
        compiler_params=params(room),
        name="weight_grad",
    )(keep, own, other)
    pieces = 4
    grad_hidden, grad_gates_t = pl.pallas_call(
        functools.partial(finish, peers, packs, pieces),
        out_shape=[shape((routed, units), BF), shape((top_count, tokens), F32)],
        in_specs=[vmem()] * (4 + len(packs)) + [anywhere()],
        out_specs=[anywhere(), vmem()],
        scratch_shapes=[pltpu.VMEM((routed, units), BF), pltpu.SemaphoreType.DMA((pieces,))],
        compiler_params=params(room),
        name="finish",
    )(low_map, pick_map, side, *raws, back, done)
    return grad_down, grad_hidden.reshape(tokens, top_count, units), grad_gates_t.T


def solution(mesh):
    in_specs = (
        P(("groups", "expert", "dp"), None),
        P(("groups", "expert", "dp"), None, None),
        P(("groups", "expert", "dp"), None),
        P(("groups", "expert", "dp"), None),
        P("expert", "dp", None),
    )
    out_specs = (
        P(("groups", "expert"), "dp", None),
        P(("groups", "expert", "dp"), None, None),
        P(("groups", "expert", "dp"), None),
    )
    return jax.shard_map(local, mesh=mesh, in_specs=in_specs, out_specs=out_specs, check_vma=False)
```
